512 devices in a mesh: grp: 32 (over x, y), dev: 16 (over z, core).
Axes of the slice: x: 4, y: 8, z: 8, core: 2. Of those that a mesh axis runs over, the one named last changes fastest.
Arguments:
- design: float32 [262144, 1024], P(('grp', 'dev')), as said below
- observed: float32 [262144], P(('grp', 'dev')), may hold values from -6 to 6
- row_weight: float32 [262144], P(('grp', 'dev')), may hold values from 0.3 to 3
- arc_of_row: int32 [262144, 1], P(('grp', 'dev')), may hold values from 0 to 31, as said below
- prior_factor: float32 [1024, 1024], P('dev'), as said below
- prior_rhs: float32 [1024], P('dev'), may hold values from -6 to 6
Outputs:
- new_factor: float32 [1024, 1024], P('dev')
- new_rhs: float32 [1024], P('dev')
The draws below stay inside these ranges and needn't reach their ends.
Inputs may be any that keep to these rules, and one draw needn't show every extreme that they name: `arc_of_row`: arc numbers count within a group of 16 devices along dev; arc a of a group is owned by the device of index a // 2 in that group. Among the rows of one device no arc stands more than 24 times. In every group the arcs of one owner stand exactly 24 times among the rows of every device of that group. `prior_factor`: upper triangular with diagonal between 1 and 2. `design`: entries below 1 in magnitude.
All inputs are finite; a program needn't handle non-finite values.
Results may differ from the reference program's by a relative error of at most 0.0013.
Values sent between devices are 32-bit elements; how exact they have to be, the bound alone decides.
No kernel may reach another device: no remote copies, remote signals or barrier semaphores. Data moves between devices by JAX's collectives and lax.ppermute only.
A program may use at most 128 MiB of HBM per device.

```python
import math
import jax
import jax.numpy as jnp
from jax import lax

P_SIZE = 1024
ROWS_DEV = 512
ARCS_DEV = 2
ARCS_GRP = 32
MOST = 24
ROWS = 262144
N_GRP = 32
N_DEV = 16


def permute_slots(piece_key):
    return jax.random.permutation(piece_key, ARCS_GRP * MOST)


def permute_rows(piece_key):
    return jax.random.permutation(piece_key, ROWS_DEV)


def arc_labels(key):
    devices = N_GRP * N_DEV
    slot_count = ARCS_GRP * MOST
    first, second, third = jax.random.split(key, 3)
    owners = jnp.repeat(jax.random.randint(first, (N_GRP,), 0, N_DEV), N_DEV)
    slot_arc = jnp.arange(slot_count, dtype=jnp.int32) // MOST
    owned = (slot_arc // ARCS_DEV)[None, :] == owners[:, None]
    ranks = jax.vmap(permute_slots)(jax.random.split(second, devices)).astype(jnp.int32)
    scores = jnp.where(owned, ranks, ranks + slot_count)
    order = jnp.argsort(scores, axis=1, stable=True)[:, :ROWS_DEV]
    chosen = (order // MOST).astype(jnp.int32)
    mixing = jax.vmap(permute_rows)(jax.random.split(third, devices))
    labels = jnp.take_along_axis(chosen, mixing, axis=1)
    return labels.reshape(devices * ROWS_DEV, 1).astype(jnp.int32)


def draw_arc_of_row(key, part):
    return arc_labels(key)


def draw_design(key, part):
    labels = arc_labels(key)[:, 0]
    key = jax.random.fold_in(key, 11)
    first, second, third, fourth, fifth = jax.random.split(key, 5)
    groups = jnp.arange(ROWS, dtype=jnp.int32) // (ROWS_DEV * N_DEV)
    global_arc = groups * ARCS_GRP + labels
    arc_total = ARCS_GRP * N_GRP
    signs = (jax.random.randint(fifth, (1, P_SIZE), 0, 2) * 2 - 1).astype(jnp.float32)
    common = jax.random.normal(first, (arc_total, P_SIZE), jnp.float32)
    rough = jax.random.normal(second, (ROWS, P_SIZE), jnp.float32)
    shared_col = signs * jnp.exp(jax.random.uniform(third, (1, P_SIZE), jnp.float32, math.log(0.6), math.log(1.4)))
    row_factor = jax.random.normal(fourth, (ROWS, 1), jnp.float32)
    shared_scale = 4.5
    values = (jnp.take(common, global_arc, axis=0) + rough + shared_scale * row_factor * shared_col) * (1.0 / math.sqrt(ROWS))
    return jnp.clip(values, -0.99, 0.99)


def draw_prior_factor(key, part):
    key = jax.random.fold_in(key, 7)
    first, second = jax.random.split(key)
    row_index = jnp.arange(P_SIZE)[:, None]
    col_index = jnp.arange(P_SIZE)[None, :]
    diag = jnp.exp(jax.random.uniform(first, (P_SIZE,), jnp.float32, 0.0, math.log(2.0)))
    offdiag = jax.random.normal(second, (P_SIZE, P_SIZE), jnp.float32) * (0.3 / math.sqrt(P_SIZE))
    upper = jnp.where(col_index > row_index, offdiag, 0.0)
    return upper + jnp.where(col_index == row_index, diag[None, :], 0.0)


def level_of(key, dims, shards, low, top_value):
    def one(dim, shards_of):
        draws = jax.random.uniform(jax.random.fold_in(jax.random.fold_in(key, 6), dim), (shards_of,), jnp.float32, low / len(shards), top_value / len(shards))
        return jnp.repeat(jnp.exp(draws), dims[dim] // shards_of).reshape((-1,) + (1,) * (len(dims) - dim - 1))

    gain = one(*shards[0])
    for cut in shards[1:]:
        gain = gain * one(*cut)
    return gain


def bell_draw(rng, shape, spread, most, cuts=(), kind=jnp.bfloat16):
    result = jax.random.normal(rng, shape, jnp.float32) * spread
    if len(cuts) > 0:
        result = level_of(rng, shape, cuts, -0.22, 0.18) * result
    return jnp.clip(result, min=-most, max=most).astype(kind)


def setup_inputs(seed: int = 0) -> dict:
    key_of = jax.random.split(jax.random.key(seed), 7)
    return {
        "design": draw_design(jax.random.fold_in(key_of[6], 71), 0),
        "observed": bell_draw(key_of[1], (ROWS,), 1.0, 6.0, ((0, 512),), jnp.float32),
        "row_weight": jnp.clip(jnp.exp(math.log(3.0) - 2.3025851 * jax.random.uniform(key_of[2], (ROWS,), jnp.float32) ** level_of(key_of[2], (ROWS,), ((0, 512),), -0.2, 0.2)), 0.3, 3.0),
        "arc_of_row": draw_arc_of_row(jax.random.fold_in(key_of[6], 71), 0),
        "prior_factor": draw_prior_factor(jax.random.fold_in(key_of[6], 71), 0),
        "prior_rhs": bell_draw(key_of[5], (P_SIZE,), 1.0, 6.0, ((0, 16),), jnp.float32),
    }


bias_prior = 1.0

def inner(left, right):
    return lax.dot_general(left.astype(jnp.float32), right.astype(jnp.float32), (((0,), (0,)), ((), ())), precision=lax.Precision.HIGHEST, preferred_element_type=jnp.float32)

def reference(design, observed, row_weight, arc_of_row, prior_factor, prior_rhs):
    rows_all = design.shape[0]
    groups = jnp.arange(rows_all, dtype=jnp.int32) // (ROWS_DEV * N_DEV)
    arc_ids = (groups * ARCS_GRP + arc_of_row[:, 0]).astype(jnp.int32)
    arc_count = ARCS_GRP * N_GRP
    weighted = row_weight[:, None] * design
    scaled_obs = row_weight * observed
    arc_sum = jax.ops.segment_sum(row_weight[:, None] * weighted, arc_ids, arc_count)
    total = jax.ops.segment_sum(row_weight * row_weight, arc_ids, arc_count) + bias_prior
    obs_sum = jax.ops.segment_sum(row_weight * scaled_obs, arc_ids, arc_count)
    gram = inner(weighted, weighted) + inner(prior_factor, prior_factor) - inner(arc_sum / total[:, None], arc_sum)
    projected = inner(weighted, scaled_obs) + inner(prior_factor, prior_rhs) - inner(arc_sum, obs_sum / total)
    lower = jnp.linalg.cholesky(gram)
    solved = lax.linalg.triangular_solve(lower, projected[:, None], left_side=True, lower=True)
    return (lower.T, solved[:, 0])
```

```python
import functools

import jax
import jax.numpy as jnp
from jax import lax
from jax.experimental import pallas as pl
from jax.experimental.pallas import tpu as pltpu
from jax.sharding import Mesh
from jax.sharding import PartitionSpec as P

f32 = jnp.float32
bf16 = jnp.bfloat16
NB = 128
bias_prior = 1.0
VMEM = pl.BlockSpec(memory_space=pltpu.VMEM)
SMEM = pl.BlockSpec(memory_space=pltpu.SMEM)


def spread(x, i):
    return jnp.broadcast_to(x[i:i+1, :], (8, x.shape[1]))

def across(x, lane):
    return jnp.broadcast_to(x[:, lane:lane+1], (8, 128))

def split(x):
    hi = x.astype(bf16)
    rest = x - hi.astype(f32)
    mid = rest.astype(bf16)
    return hi, mid, (rest - mid.astype(f32)).astype(bf16)

def left_stack(x, axis):
    h, m, l = split(x)
    return jnp.concatenate([h, h, m, m, h, l], axis=axis)

def right_stack(x, axis):
    h, m, l = split(x)
    return jnp.concatenate([h, m, h, m, l, h], axis=axis)

def dot(a, b, ca, cb):
    return lax.dot_general(a, b, (((ca,), (cb,)), ((), ())), preferred_element_type=f32)

def factor_block(rows):
    sub = lax.broadcasted_iota(jnp.int32, (8, 128), 0)
    lane = lax.broadcasted_iota(jnp.int32, (8, 128), 1)
    n = 16
    left = list(rows)
    right = [jnp.where(lane == sub + 8 * b, 1.0, 0.0).astype(f32) for b in range(n)]
    up, inv = [], []
    for b in range(n):
        near = [c for c in (b, b + 1, b + 2) if c < n]
        col = [[across(left[c], 8 * b + j) for c in near] for j in range(8)]
        x, y = left[b], right[b]
        diag = jnp.zeros((8, 128), f32)
        mults = []
        for j in range(8):
            piv = spread(col[j][0], j)
            if j < 7:
                head = spread(col[j + 1][0], j)
                pre = col[j][0] * head
            q = 1.0 / piv
            diag = jnp.where(sub == j, piv, diag)
            if j < 7:
                col[j + 1][0] = col[j + 1][0] - pre * q
                factor = head * q
                for t in range(1, len(near)):
                    col[j + 1][t] = col[j + 1][t] - col[j][t] * factor
                for k in range(j + 2, 8):
                    factor = spread(col[k][0], j) * q
                    for t in range(len(near)):
                        col[k][t] = col[k][t] - col[j][t] * factor
                m = jnp.where(sub > j, col[j][0] * q, 0.0)
                x = x - m * spread(x, j)
                y = y - m * spread(y, j)
            mults.append([col[j][t] * q for t in range(1, len(near))])
        for t in range(1, len(near)):
            c = near[t]
            dx = [mults[j][t - 1] * spread(x, j) for j in range(8)]
            dy = [mults[j][t - 1] * spread(y, j) for j in range(8)]
            while len(dx) > 1:
                dx = [dx[i] + dx[i + 1] for i in range(0, len(dx), 2)]
                dy = [dy[i] + dy[i + 1] for i in range(0, len(dy), 2)]
            left[c] = left[c] - dx[0]
            right[c] = right[c] - dy[0]
        r = lax.rsqrt(diag)
        x = x * r
        y = y * r
        up.append(x); inv.append(y)
        if b + 3 < n:
            z = jnp.concatenate([x, y], axis=1)
            h = z.astype(bf16).astype(f32)
            m = (z - h).astype(bf16).astype(f32)
            l = z - h - m
            lhs = jnp.concatenate([p[:, :128] for p in (h, h, m, m, h, l)], axis=0).astype(bf16)
            rhs = jnp.concatenate([h, m, h, m, l, h], axis=0).astype(bf16)
            upd = dot(lhs, rhs, 0, 0)
            for c in range(b + 3, n):
                left[c] = left[c] - upd[8 * c:8 * c + 8, :128]
                right[c] = right[c] - upd[8 * c:8 * c + 8, 128:]
    return up, inv

def chol_body(a_ref, out_ref, nblk, width):
    for k in range(nblk):
        r0 = k * NB
        rows = [a_ref[r0 + 8*b: r0 + 8*b + 8, r0:r0 + NB] for b in range(16)]
        up, inv = factor_block(rows)
        li = lax.broadcasted_iota(jnp.int32, (NB, NB), 1)
        si = lax.broadcasted_iota(jnp.int32, (NB, NB), 0)
        out_ref[r0:r0 + NB, r0:r0 + NB] = jnp.where(li >= si, jnp.concatenate(up, axis=0), 0.0)
        t = left_stack(jnp.concatenate(inv, axis=0), 1)
        if r0 > 0:
            out_ref[r0:r0 + NB, 0:r0] = jnp.zeros((NB, r0), f32)
        pieces = []
        lo = r0 + NB
        while lo < width:
            hi = min(lo + 2 * NB - lo % (2 * NB), width)
            p = dot(t, right_stack(a_ref[r0:r0 + NB, lo:hi], 0), 1, 0)
            out_ref[r0:r0 + NB, lo:hi] = p
            pieces.append((lo, hi, p))
            lo = hi
        if k + 1 < nblk:
            full = jnp.concatenate([left_stack(p.T, 1) for lo, hi, p in pieces if lo < nblk * NB], axis=0)
            for lo, hi, p in pieces:
                top, end = r0 + NB, min(hi, nblk * NB)
                a_ref[top:end, lo:hi] = a_ref[top:end, lo:hi] - dot(full[:end - top], right_stack(p, 0), 1, 0)


def exact(a, b):
    return lax.dot_general(
        a, b, (((1,), (0,)), ((), ())), precision=lax.Precision.HIGHEST, preferred_element_type=f32
    )


def blocks_of(nblk):
    return [(i, j) for i in range(nblk) for j in range(i, nblk)]


def arcs_kernel(design_ref, weight_ref, obs_ref, arc_ref, out_ref):
    rows, width = design_ref.shape
    arcs = out_ref.shape[0]
    w = weight_ref[...]
    number = lax.broadcasted_iota(jnp.int32, (arcs, rows), 0)
    member = jnp.where(number == arc_ref[...], w * w, 0.0)
    out_ref[:, :width] = exact(member, design_ref[...])
    total = jnp.sum(member, axis=1, keepdims=True)
    obs = jnp.sum(member * obs_ref[...], axis=1, keepdims=True)
    lane = lax.broadcasted_iota(jnp.int32, (arcs, NB), 1)
    out_ref[:, width:] = jnp.where(lane == 0, obs, jnp.where(lane == 1, total, 0.0))


def gram_kernel(
    where_ref, design_ref, weight_ref, obs_ref, prior_ref, prhs_ref, keep_ref, send_ref, rows_ref, both_ref
):
    rows, width = design_ref.shape
    prows = prior_ref.shape[0]
    nblk = width // NB
    core = where_ref[0]
    include = where_ref[1].astype(f32)
    w = weight_ref[...]
    for r in range(0, rows, NB):
        column = jnp.broadcast_to(w[:, r:r + NB], (NB, NB)).T
        for c in range(0, width, NB):
            rows_ref[r:r + NB, c:c + NB] = design_ref[r:r + NB, c:c + NB] * column
    rows_ref[rows:rows + prows, :] = prior_ref[...] * include
    deep = rows + prows
    wobs = jnp.concatenate([w * obs_ref[...], prhs_ref[...]], axis=1)
    p = exact(jnp.broadcast_to(wobs, (8, deep)), rows_ref[...])
    order = blocks_of(nblk)
    half = len(order) // 2
    tall = []
    for i in range(nblk):
        z = rows_ref[:, i * NB:(i + 1) * NB]
        turned = jnp.concatenate([z[r:min(r + NB, deep)].T for r in range(0, deep, NB)], axis=1)
        h = turned.astype(bf16)
        m = (turned - h.astype(f32)).astype(bf16)
        tall.append(jnp.concatenate([h, h, m], axis=1))
    tall = jnp.concatenate(tall, axis=0)
    step = 2 * NB
    for lo in range(0, width, step):
        z = rows_ref[:, lo:lo + step]
        h = z.astype(bf16)
        m = (z - h.astype(f32)).astype(bf16)
        flat = jnp.concatenate([h, m, h], axis=0)
        g = dot(tall[:lo + step], flat, 1, 0)
        for i in range((lo + step) // NB):
            for j in (lo // NB, lo // NB + 1):
                if j >= i:
                    t = order.index((i, j))
                    both_ref[t // half, (t % half) * NB:(t % half + 1) * NB, :] = g[
                        i * NB:(i + 1) * NB, (j * NB - lo):(j * NB - lo) + NB
                    ]
    for r in range(2 * nblk):
        t = order.index((r // nblk, r // nblk))
        row = t * NB + NB - 8 + r % nblk
        both_ref[row // (half * NB), row % (half * NB):row % (half * NB) + 1, 0:64] = p[0:1, r * 64:(r + 1) * 64]
    keep_ref[...] = both_ref[core]
    send_ref[...] = both_ref[1 - core]


def pair_kernel(where_ref, mine_ref, got_ref, arcs_ref, out_ref):
    width = arcs_ref.shape[1] - NB
    nblk = width // NB
    order = blocks_of(nblk)
    half = len(order) // 2
    core = where_ref[0]
    s = arcs_ref[0:8, :]
    for r in range(8, arcs_ref.shape[0], 8):
        s = s + arcs_ref[r:r + 8, :]
    s = s + pltpu.roll(s, 4, 0)
    total = s[:, width + 1:width + 2] + bias_prior
    sub = lax.broadcasted_iota(jnp.int32, s.shape, 0)
    b = jnp.where(sub < 4, s * lax.rsqrt(jnp.broadcast_to(total, s.shape)), 0.0)
    obs = b[:, width:width + 1]
    p = jnp.sum(b[:, :width] * obs, axis=0, keepdims=True)
    h = b.astype(bf16).astype(f32)
    m = (b - h).astype(bf16).astype(f32)
    l = b - h - m
    lhs = jnp.concatenate([h, h, m, m, h, l], axis=0).astype(bf16)
    rhs = jnp.concatenate([h, m, h, m, l, h], axis=0).astype(bf16)

    def one(side):
        for t in range(half):
            i, j = order[side * half + t]
            part = dot(lhs[:, i * NB:(i + 1) * NB], rhs[:, j * NB:(j + 1) * NB], 0, 0)
            if i == j and i < 2:
                mine_row = [
                    jnp.concatenate([p[:, r * 64:(r + 1) * 64], part[NB - 8 + r % nblk:NB - 8 + r % nblk + 1, 64:]], axis=1)
                    for r in range(i * nblk, (i + 1) * nblk)
                ]
                part = jnp.concatenate([part[:NB - 8]] + mine_row, axis=0)
            out_ref[t * NB:(t + 1) * NB, :] = mine_ref[t * NB:(t + 1) * NB, :] + got_ref[t * NB:(t + 1) * NB, :] - part

    pl.when(core == 0)(functools.partial(one, 0))
    pl.when(core == 1)(functools.partial(one, 1))


def factor_kernel(where_ref, mine_ref, other_ref, out_ref, rhs_ref, a_ref, u_ref):
    n = u_ref.shape[0]
    nblk = n // NB
    order = blocks_of(nblk)
    half = len(order) // 2
    core = where_ref[0]
    first = core == 0
    for t, (i, j) in enumerate(order):
        rows = pl.ds((t % half) * NB, NB)
        a, b = (mine_ref, other_ref) if t < half else (other_ref, mine_ref)
        a_ref[i * NB:(i + 1) * NB, j * NB:(j + 1) * NB] = jnp.where(first, a[rows, :], b[rows, :])
    lane = lax.broadcasted_iota(jnp.int32, (NB, NB), 1)
    for k in range(nblk):
        d = (2 * k // nblk) * NB
        r = d + NB - 8 + (2 * k) % nblk
        line = jnp.concatenate([a_ref[r:r + 1, d:d + 64], a_ref[r + 1:r + 2, d:d + 64]], axis=1)
        a_ref[k * NB:(k + 1) * NB, n:] = jnp.where(lane == 0, jnp.broadcast_to(line, (NB, NB)).T, 0.0)
    chol_body(a_ref, u_ref, nblk, n + NB)
    share = out_ref.shape[0]
    mine = pl.ds(pl.multiple_of(where_ref[1] * share, share), share)
    out_ref[...] = u_ref[mine, :n]
    rhs_ref[...] = u_ref[mine, n:].T[0:1, :]


def call(kernel, name, where, args, outs, scratch, grant):
    return pl.pallas_call(
        kernel,
        out_shape=outs,
        in_specs=([SMEM] if where is not None else []) + [VMEM] * len(args),
        out_specs=jax.tree.map(lambda _: VMEM, outs),
        scratch_shapes=scratch,
        compiler_params=pltpu.CompilerParams(vmem_limit_bytes=grant * 2**20),
        name=name,
    )(*(() if where is None else (where,)), *args)


def like(*shape):
    return jax.ShapeDtypeStruct(shape, f32)


def on_device(design, observed, row_weight, arc_of_row, prior_factor, prior_rhs):
    rows, width = design.shape
    prows = prior_factor.shape[0]
    nx, ny, nz, nc = (lax.axis_size(a) for a in ("x", "y", "z", "core"))
    core, z = lax.axis_index("core"), lax.axis_index("z")
    arcs = 2 * nz * nc
    nblk = width // NB
    half = len(blocks_of(nblk)) // 2 * NB
    include = ((lax.axis_index("x") == 0) & (lax.axis_index("y") == 0)).astype(jnp.int32)
    weight = row_weight.reshape(1, rows)
    obs = observed.reshape(1, rows)
    arc = arc_of_row.reshape(1, rows)
    partial = call(arcs_kernel, "arcs", None, (design, weight, obs, arc), like(arcs, width + NB), [], 32)
    spread_arcs = jnp.repeat(partial.reshape(nz, 2 * nc, width + NB), nc, axis=0)
    owned = lax.all_to_all(spread_arcs, ("z", "core"), 0, 0, tiled=True)
    keep, send = call(
        gram_kernel,
        "gram",
        jnp.stack([core, include]).astype(jnp.int32),
        (design, weight, obs, prior_factor, (prior_rhs * include.astype(f32)).reshape(1, prows)),
        (like(half, NB), like(half, NB)),
        [pltpu.VMEM((rows + prows, width), f32), pltpu.VMEM((2, half, NB), f32)],
        48,
    )
    swap = [(i, 1 - i) for i in range(nc)]
    got = lax.ppermute(send, "core", swap)
    where = jnp.stack([core, z * nc + core]).astype(jnp.int32)
    v = call(
        pair_kernel, "pair", where, (keep, got, owned.reshape(-1, width + NB)), like(half, NB), [], 32
    )
    v = lax.all_to_all(v.reshape(nx, half // nx, NB), "x", 0, 0, tiled=True).sum(0)
    v = lax.all_to_all(v.reshape(ny, half // nx // ny, NB), "y", 0, 0, tiled=True).sum(0)
    v = lax.all_to_all(jnp.broadcast_to(v, (nz, *v.shape)), "z", 0, 0, tiled=True).sum(0)
    v = lax.all_to_all(jnp.broadcast_to(v, (ny, *v.shape)), "y", 0, 0, tiled=True)
    v = v.reshape(half // nx, NB)
    v = lax.all_to_all(jnp.broadcast_to(v, (nx, *v.shape)), "x", 0, 0, tiled=True)
    v = v.reshape(half, NB)
    other = lax.ppermute(v, "core", swap)
    factor, rhs = call(
        factor_kernel,
        "factor",
        where,
        (v, other),
        (like(prows, width), like(1, prows)),
        [pltpu.VMEM((width, width + NB), f32), pltpu.VMEM((width, width + NB), f32)],
        48,
    )
    return factor, rhs.reshape(prows)


def solution(mesh):
    fine = Mesh(mesh.devices.reshape(4, 8, 8, 2), ("x", "y", "z", "core"))
    every = ("x", "y", "z", "core")
    placed = (
        P(every, None),
        P(every),
        P(every),
        P(every, None),
        P(("z", "core"), None),
        P(("z", "core")),
    )
    return jax.shard_map(
        on_device,
        mesh=fine,
        in_specs=placed,
        out_specs=(P(("z", "core"), None), P(("z", "core"))),
        check_vma=False,
    )
```

```python
import functools

import jax
import jax.numpy as jnp
from jax import lax
from jax.experimental import pallas as pl
from jax.experimental.pallas import tpu as pltpu
from jax.sharding import Mesh
from jax.sharding import PartitionSpec as P

f32 = jnp.float32
bf16 = jnp.bfloat16
NB = 128
bias_prior = 1.0
VMEM = pl.BlockSpec(memory_space=pltpu.VMEM)
FAR = pl.BlockSpec(memory_space=pltpu.HBM)
SMEM = pl.BlockSpec(memory_space=pltpu.SMEM)


def spread(x, i):
    return jnp.broadcast_to(x[i:i+1, :], (8, x.shape[1]))

def across(x, lane):
    return jnp.broadcast_to(x[:, lane:lane+1], (8, 128))

def split(x):
    hi = x.astype(bf16)
    rest = x - hi.astype(f32)
    mid = rest.astype(bf16)
    return hi, mid, (rest - mid.astype(f32)).astype(bf16)

def left_stack(x, axis):
    h, m, l = split(x)
    return jnp.concatenate([h, h, m, m, h, l], axis=axis)

def right_stack(x, axis):
    h, m, l = split(x)
    return jnp.concatenate([h, m, h, m, l, h], axis=axis)

def dot(a, b, ca, cb):
    return lax.dot_general(a, b, (((ca,), (cb,)), ((), ())), preferred_element_type=f32)

def factor_block(rows, tall=2, ahead=2):
    sub = lax.broadcasted_iota(jnp.int32, (8, 128), 0)
    lane = lax.broadcasted_iota(jnp.int32, (8, 128), 1)
    n = 16
    left = list(rows)
    up, inv = [], []
    for b in range(0, n, tall):
        own = list(range(b, b + tall))
        near = list(range(b + tall, min(b + tall + ahead, n)))
        steps = 8 * tall
        col = [{c: across(left[c], 8 * b + j) for c in own[j // 8:] + near} for j in range(steps)]
        x = {c: left[c] for c in own}
        y = {c: jnp.where(lane == sub + 8 * c, 1.0, 0.0) for c in own}
        diag = {c: jnp.ones((8, 128), f32) for c in own}
        mults = []
        for j in range(steps):
            home = own[j // 8]
            q = 1.0 / spread(col[j][home], j % 8)
            diag[home] = jnp.where(sub == j % 8, q, diag[home])
            scaled = {c: col[j][c] * q for c in col[j]}
            for k in range(j + 1, steps):
                kh = own[k // 8]
                head = spread(col[j][kh], k % 8)
                for c in col[k]:
                    col[k][c] = col[k][c] - scaled[c] * head
            sx, sy = spread(x[home], j % 8), spread(y[home], j % 8)
            for c in own[j // 8:]:
                m = jnp.where(sub > j % 8, scaled[c], 0.0) if c == home else scaled[c]
                x[c] = x[c] - m * sx
                y[c] = y[c] - m * sy
            mults.append(scaled)
        done = (lane >= 8 * b) & (lane < 8 * (b + tall))
        z = {c: jnp.where(done, y[c], x[c]) for c in own}
        if near:
            lines = [spread(z[own[j // 8]], j % 8) for j in range(steps)]
        for c in near:
            dx = [mults[j][c] * lines[j] for j in range(steps)]
            while len(dx) > 1:
                dx = [dx[i] + dx[i + 1] for i in range(0, len(dx), 2)]
            left[c] = jnp.where(done, 0.0, left[c]) - dx[0]
        for c in own:
            r = jnp.sqrt(diag[c])
            up.append(x[c] * r)
            z[c] = z[c] * r
            inv.append(jnp.where(lane < 8 * (b + tall), z[c], 0.0))
        after = b + tall + ahead
        if after < n:
            w = jnp.concatenate([z[c] for c in own], axis=0)
            h = w.astype(bf16).astype(f32)
            m = (w - h).astype(bf16).astype(f32)
            l = w - h - m
            lhs = jnp.concatenate([h, h, m, m, h, l], axis=0).astype(bf16)
            rhs = jnp.concatenate([h, m, h, m, l, h], axis=0).astype(bf16)
            upd = dot(lhs, rhs, 0, 0)
            for c in range(after, n):
                left[c] = jnp.where(done, 0.0, left[c]) - upd[8 * c:8 * c + 8, :]
    return up, inv

def chol_body(a_ref, out_ref, nblk, width):
    for k in range(nblk):
        r0 = k * NB
        rows = [a_ref[r0 + 8*b: r0 + 8*b + 8, r0:r0 + NB] for b in range(16)]
        up, inv = factor_block(rows)
        li = lax.broadcasted_iota(jnp.int32, (NB, NB), 1)
        si = lax.broadcasted_iota(jnp.int32, (NB, NB), 0)
        out_ref[r0:r0 + NB, r0:r0 + NB] = jnp.where(li >= si, jnp.concatenate(up, axis=0), 0.0)
        t = left_stack(jnp.concatenate(inv, axis=0), 1)
        if r0 > 0:
            out_ref[r0:r0 + NB, 0:r0] = jnp.zeros((NB, r0), f32)
        pieces = []
        lo = r0 + NB
        while lo < width:
            hi = min(lo + 2 * NB - lo % (2 * NB), width)
            p = dot(t, right_stack(a_ref[r0:r0 + NB, lo:hi], 0), 1, 0)
            out_ref[r0:r0 + NB, lo:hi] = p
            pieces.append((lo, hi, p))
            lo = hi
        if k + 1 < nblk:
            full = jnp.concatenate([left_stack(p.T, 1) for lo, hi, p in pieces if lo < nblk * NB], axis=0)
            for lo, hi, p in pieces:
                top, end = r0 + NB, min(hi, nblk * NB)
                a_ref[top:end, lo:hi] = a_ref[top:end, lo:hi] - dot(full[:end - top], right_stack(p, 0), 1, 0)


def exact(a, b):
    return lax.dot_general(
        a, b, (((1,), (0,)), ((), ())), precision=lax.Precision.HIGHEST, preferred_element_type=f32
    )


def blocks_of(nblk):
    return [(i, j) for i in range(nblk) for j in range(i, nblk)]


def fetch(pairs, sem):
    copies = [pltpu.make_async_copy(src, dst, sem.at[i]) for i, (src, dst) in enumerate(pairs)]
    for copy in copies:
        copy.start()
    return copies


def row_parts(rows):
    return [pl.ds(r, NB) for r in range(0, rows, NB)]


def arcs_kernel(design_hbm, weight_hbm, obs_hbm, arc_hbm, out_ref, design_ref, weight_ref, obs_ref, arc_ref, sem):
    rows, width = design_ref.shape
    arcs = out_ref.shape[0]
    parts = row_parts(rows)
    copies = fetch(
        [(weight_hbm, weight_ref), (arc_hbm, arc_ref), (obs_hbm, obs_ref)]
        + [(design_hbm.at[p], design_ref.at[p]) for p in parts],
        sem,
    )
    for copy in copies[:3]:
        copy.wait()
    w = weight_ref[...]
    row = lax.broadcasted_iota(jnp.int32, (arcs, rows), 0)
    member = jnp.where((row // 8) * 4 + row % 4 == arc_ref[...], w * w, 0.0)
    total = jnp.sum(member, axis=1, keepdims=True)
    obs = jnp.sum(member * obs_ref[...], axis=1, keepdims=True)
    lane = lax.broadcasted_iota(jnp.int32, (arcs, NB), 1)
    out_ref[:, width:] = jnp.where(lane == 0, obs, jnp.where(lane == 1, total, 0.0))
    sums = None
    for n, p in enumerate(parts):
        copies[3 + n].wait()
        more = exact(member[:, n * NB:(n + 1) * NB], design_ref[p, :])
        sums = more if sums is None else sums + more
    out_ref[:, :width] = sums


def half_kernel(mine, where_ref, tall_ref, flat_ref, p_ref, out_ref):
    width = flat_ref.shape[1]
    deep = flat_ref.shape[0] // 2
    nblk = width // NB
    order = blocks_of(nblk)
    half = len(order) // 2
    core = where_ref[0]

    def one(side):
        wanted = order[side * half:(side + 1) * half]
        for lo in range(0, nblk, 2):
            tops = sorted({i for i, j in wanted if j in (lo, lo + 1)})
            if not tops:
                continue
            cols = sorted({j for i, j in wanted if j in (lo, lo + 1)})
            c0, c1 = cols[0] * NB, cols[-1] * NB + NB
            r0, r1 = tops[0] * NB, tops[-1] * NB + NB
            g = dot(tall_ref[r0:r1, :], flat_ref[:, c0:c1], 1, 0)
            g = g + dot(tall_ref[r0:r1, :deep], flat_ref[deep:, c0:c1], 1, 0)
            for j in cols:
                for i in tops:
                    if (i, j) in wanted:
                        block = g[i * NB - r0:i * NB - r0 + NB, j * NB - c0:j * NB - c0 + NB]
                        at = wanted.index((i, j)) * NB
                        if i == j and i < 2:
                            corner = [p_ref[0:1, r * 64:(r + 1) * 64] for r in range(i * nblk, (i + 1) * nblk)]
                            corner = jnp.concatenate(corner, axis=0)
                            last = jnp.concatenate([corner, block[NB - 8:, 64:]], axis=1)
                            block = jnp.concatenate([block[:NB - 8], last], axis=0)
                        out_ref[at:at + NB, :] = block

    pl.when(core == (0 if mine else 1))(functools.partial(one, 0))
    pl.when(core == (1 if mine else 0))(functools.partial(one, 1))


def first_kernel(
    where_ref, design_ref, weight_ref, obs_ref, prior_ref, prhs_ref, after_ref, out_ref, tall_ref, flat_ref, p_ref
):
    rows, width = design_ref.shape
    prows = prior_ref.shape[0]
    deep = tall_ref.shape[1] // 2
    include = where_ref[1].astype(f32)
    w = weight_ref[...]
    wobs = jnp.broadcast_to(w * w * obs_ref[...], (8, rows))

    def place(r, z):
        for c in range(0, width, NB):
            h = z[:, c:c + NB].astype(bf16)
            m = (z[:, c:c + NB] - h.astype(f32)).astype(bf16)
            flat_ref[r:r + NB, c:c + NB] = m
            flat_ref[deep + r:deep + r + NB, c:c + NB] = h
            turned = z[:, c:c + NB].T
            h = turned.astype(bf16)
            tall_ref[c:c + NB, r:r + NB] = h
            tall_ref[c:c + NB, deep + r:deep + r + NB] = (turned - h.astype(f32)).astype(bf16)

    for r in range(0, rows, NB):
        column = jnp.broadcast_to(w[:, r:r + NB], (NB, NB)).T
        place(r, design_ref[r:r + NB, :] * jnp.concatenate([column] * (width // NB), axis=1))
    prior = prior_ref[...] * include
    place(rows, jnp.concatenate([prior, jnp.zeros((NB - prows, width), f32)], axis=0))
    p_ref[...] = exact(wobs, design_ref[...]) + exact(jnp.broadcast_to(prhs_ref[...], (8, prows)), prior)
    half_kernel(False, where_ref, tall_ref, flat_ref, p_ref, out_ref)


def pair_kernel(where_ref, mine_ref, got_ref, arcs_ref, out_ref):
    width = arcs_ref.shape[1] - NB
    nblk = width // NB
    order = blocks_of(nblk)
    half = len(order) // 2
    core = where_ref[0]
    s = arcs_ref[0:8, :]
    for r in range(8, arcs_ref.shape[0], 8):
        s = s + arcs_ref[r:r + 8, :]
    s = s + pltpu.roll(s, 4, 0)
    total = s[:, width + 1:width + 2] + bias_prior
    sub = lax.broadcasted_iota(jnp.int32, s.shape, 0)
    b = jnp.where(sub < 4, s * lax.rsqrt(jnp.broadcast_to(total, s.shape)), 0.0)
    obs = b[:, width:width + 1]
    p = jnp.sum(b[:, :width] * obs, axis=0, keepdims=True)
    h = b.astype(bf16).astype(f32)
    m = (b - h).astype(bf16).astype(f32)
    l = b - h - m
    lhs = jnp.concatenate([h, h, m, m, h, l], axis=0).astype(bf16)
    rhs = jnp.concatenate([h, m, h, m, l, h], axis=0).astype(bf16)

    def one(side):
        for t in range(half):
            i, j = order[side * half + t]
            part = dot(lhs[:, i * NB:(i + 1) * NB], rhs[:, j * NB:(j + 1) * NB], 0, 0)
            if i == j and i < 2:
                mine_row = [
                    jnp.concatenate([p[:, r * 64:(r + 1) * 64], part[NB - 8 + r % nblk:NB - 8 + r % nblk + 1, 64:]], axis=1)
                    for r in range(i * nblk, (i + 1) * nblk)
                ]
                part = jnp.concatenate([part[:NB - 8]] + mine_row, axis=0)
            out_ref[t * NB:(t + 1) * NB, :] = mine_ref[t * NB:(t + 1) * NB, :] + got_ref[t * NB:(t + 1) * NB, :] - part

    pl.when(core == 0)(functools.partial(one, 0))
    pl.when(core == 1)(functools.partial(one, 1))


def factor_kernel(where_ref, mine_ref, other_ref, out_ref, rhs_ref, a_ref, u_ref):
    n = u_ref.shape[0]
    nblk = n // NB
    order = blocks_of(nblk)
    half = len(order) // 2
    core = where_ref[0]
    first = core == 0
    for t, (i, j) in enumerate(order):
        rows = pl.ds((t % half) * NB, NB)
        a, b = (mine_ref, other_ref) if t < half else (other_ref, mine_ref)
        a_ref[i * NB:(i + 1) * NB, j * NB:(j + 1) * NB] = jnp.where(first, a[rows, :], b[rows, :])
    lane = lax.broadcasted_iota(jnp.int32, (NB, NB), 1)
    for k in range(nblk):
        d = (2 * k // nblk) * NB
        r = d + NB - 8 + (2 * k) % nblk
        line = jnp.concatenate([a_ref[r:r + 1, d:d + 64], a_ref[r + 1:r + 2, d:d + 64]], axis=1)
        a_ref[k * NB:(k + 1) * NB, n:] = jnp.where(lane == 0, jnp.broadcast_to(line, (NB, NB)).T, 0.0)
    chol_body(a_ref, u_ref, nblk, n + NB)
    share = out_ref.shape[0]
    mine = pl.ds(pl.multiple_of(where_ref[1] * share, share), share)
    out_ref[...] = u_ref[mine, :n]
    rhs_ref[...] = u_ref[mine, n:].T[0:1, :]


def call(kernel, name, where, args, outs, scratch, grant, far=False, cost=None):
    return pl.pallas_call(
        kernel,
        out_shape=outs,
        in_specs=([SMEM] if where is not None else []) + [FAR if far else VMEM] * len(args),
        out_specs=jax.tree.map(lambda _: VMEM, outs),
        scratch_shapes=scratch,
        compiler_params=pltpu.CompilerParams(vmem_limit_bytes=grant * 2**20),
        cost_estimate=cost,
        name=name,
    )(*(() if where is None else (where,)), *args)


def like(*shape):
    return jax.ShapeDtypeStruct(shape, f32)


def on_device(design, observed, row_weight, arc_of_row, prior_factor, prior_rhs):
    rows, width = design.shape
    prows = prior_factor.shape[0]
    nx, ny, nz, nc = (lax.axis_size(a) for a in ("x", "y", "z", "core"))
    core, z = lax.axis_index("core"), lax.axis_index("z")
    arcs = 2 * nz * nc
    nblk = width // NB
    half = len(blocks_of(nblk)) // 2 * NB
    include = ((lax.axis_index("x") == 0) & (lax.axis_index("y") == 0)).astype(jnp.int32)
    weight = row_weight.reshape(1, rows)
    obs = observed.reshape(1, rows)
    arc = arc_of_row.reshape(1, rows)
    nparts = rows // NB
    deep = rows + NB
    here = jnp.stack([core, include]).astype(jnp.int32)
    partial = call(
        arcs_kernel,
        "arcs",
        None,
        (design, weight, obs, arc),
        like(2 * arcs, width + NB),
        [
            pltpu.VMEM((rows, width), f32),
            pltpu.VMEM((1, rows), f32),
            pltpu.VMEM((1, rows), f32),
            pltpu.VMEM((1, rows), jnp.int32),
            pltpu.SemaphoreType.DMA((3 + nparts,)),
        ],
        56,
        far=True,
    )
    owned = lax.all_to_all(partial.reshape(nz * nc, 2 * nc, width + NB), ("z", "core"), 0, 0, tiled=True)
    work = pl.CostEstimate(flops=2 * 10**11, bytes_accessed=10**7, transcendentals=0)
    send, tall, flat, p = call(
        first_kernel,
        "first",
        here,
        (design, weight, obs, prior_factor, prior_rhs.reshape(1, prows), partial),
        (
            like(half, NB),
            pltpu.VMEM((width, 2 * deep), bf16),
            pltpu.VMEM((2 * deep, width), bf16),
            pltpu.VMEM((8, width), f32),
        ),
        [],
        20,
        cost=work,
    )
    keep = call(
        functools.partial(half_kernel, True), "keep", here, (tall, flat, p), pltpu.VMEM((half, NB), f32), [], 20, cost=work
    )
    swap = [(i, 1 - i) for i in range(nc)]
    got = lax.ppermute(send, "core", swap)
    where = jnp.stack([core, z * nc + core]).astype(jnp.int32)
    v = call(
        pair_kernel, "pair", where, (keep, got, owned.reshape(-1, width + NB)), like(half, NB), [], 32
    )
    v = lax.all_to_all(v.reshape(nx, half // nx, NB), "x", 0, 0, tiled=True).sum(0)
    plane = ny * nz
    v = lax.all_to_all(v.reshape(plane, 1, v.size // plane), ("y", "z"), 0, 0, tiled=True).sum(0)
    v = lax.all_to_all(jnp.broadcast_to(v, (plane, *v.shape)), ("y", "z"), 0, 0, tiled=True)
    v = v.reshape(half // nx, NB)
    v = lax.all_to_all(jnp.broadcast_to(v, (nx, *v.shape)), "x", 0, 0, tiled=True)
    v = v.reshape(half, NB)
    other = lax.ppermute(v, "core", swap)
    factor, rhs = call(
        factor_kernel,
        "factor",
        where,
        (v, other),
        (like(prows, width), like(1, prows)),
        [pltpu.VMEM((width, width + NB), f32), pltpu.VMEM((width, width + NB), f32)],
        32,
    )
    return factor, rhs.reshape(prows)


def solution(mesh):
    fine = Mesh(mesh.devices.reshape(4, 8, 8, 2), ("x", "y", "z", "core"))
    every = ("x", "y", "z", "core")
    placed = (
        P(every, None),
        P(every),
        P(every),
        P(every, None),
        P(("z", "core"), None),
        P(("z", "core")),
    )
    return jax.shard_map(
        on_device,
        mesh=fine,
        in_specs=placed,
        out_specs=(P(("z", "core"), None), P(("z", "core"))),
        check_vma=False,
    )
```

```python
import functools

import jax
import jax.numpy as jnp
from jax import lax
from jax.experimental import pallas as pl
from jax.experimental.pallas import tpu as pltpu
from jax.sharding import Mesh
from jax.sharding import PartitionSpec as P

f32 = jnp.float32
bf16 = jnp.bfloat16
NB = 128
bias_prior = 1.0
VMEM = pl.BlockSpec(memory_space=pltpu.VMEM)
FAR = pl.BlockSpec(memory_space=pltpu.HBM)
SMEM = pl.BlockSpec(memory_space=pltpu.SMEM)


def spread(x, i):
    return jnp.broadcast_to(x[i:i+1, :], (8, x.shape[1]))

def across(x, lane):
    return jnp.broadcast_to(x[:, lane:lane+1], (8, 128))

def split(x):
    hi = x.astype(bf16)
    rest = x - hi.astype(f32)
    mid = rest.astype(bf16)
    return hi, mid, (rest - mid.astype(f32)).astype(bf16)

def left_stack(x, axis):
    h, m, l = split(x)
    return jnp.concatenate([h, h, m, m, h, l], axis=axis)

def right_stack(x, axis):
    h, m, l = split(x)
    return jnp.concatenate([h, m, h, m, l, h], axis=axis)

def dot(a, b, ca, cb):
    return lax.dot_general(a, b, (((ca,), (cb,)), ((), ())), preferred_element_type=f32)

def factor_block(rows, tall=2, ahead=2):
    sub = lax.broadcasted_iota(jnp.int32, (8, 128), 0)
    lane = lax.broadcasted_iota(jnp.int32, (8, 128), 1)
    n = 16
    left = list(rows)
    up, inv = [], []
    for b in range(0, n, tall):
        own = list(range(b, b + tall))
        near = list(range(b + tall, min(b + tall + ahead, n)))
        steps = 8 * tall
        col = [{c: across(left[c], 8 * b + j) for c in own[j // 8:] + near} for j in range(steps)]
        x = {c: left[c] for c in own}
        y = {c: jnp.where(lane == sub + 8 * c, 1.0, 0.0) for c in own}
        diag = {c: jnp.ones((8, 128), f32) for c in own}
        mults = []
        for j in range(steps):
            home = own[j // 8]
            q = 1.0 / spread(col[j][home], j % 8)
            diag[home] = jnp.where(sub == j % 8, q, diag[home])
            scaled = {c: col[j][c] * q for c in col[j]}
            for k in range(j + 1, steps):
                kh = own[k // 8]
                head = spread(col[j][kh], k % 8)
                for c in col[k]:
                    col[k][c] = col[k][c] - scaled[c] * head
            sx, sy = spread(x[home], j % 8), spread(y[home], j % 8)
            for c in own[j // 8:]:
                m = jnp.where(sub > j % 8, scaled[c], 0.0) if c == home else scaled[c]
                x[c] = x[c] - m * sx
                y[c] = y[c] - m * sy
            mults.append(scaled)
        done = (lane >= 8 * b) & (lane < 8 * (b + tall))
        z = {c: jnp.where(done, y[c], x[c]) for c in own}
        if near:
            lines = [spread(z[own[j // 8]], j % 8) for j in range(steps)]
        for c in near:
            dx = [mults[j][c] * lines[j] for j in range(steps)]
            while len(dx) > 1:
                dx = [dx[i] + dx[i + 1] for i in range(0, len(dx), 2)]
            left[c] = jnp.where(done, 0.0, left[c]) - dx[0]
        for c in own:
            r = jnp.sqrt(diag[c])
            up.append(x[c] * r)
            z[c] = z[c] * r
            inv.append(jnp.where(lane < 8 * (b + tall), z[c], 0.0))
        after = b + tall + ahead
        if after < n:
            w = jnp.concatenate([z[c] for c in own], axis=0)
            h = w.astype(bf16).astype(f32)
            m = (w - h).astype(bf16).astype(f32)
            l = w - h - m
            lhs = jnp.concatenate([h, h, m, m, h, l], axis=0).astype(bf16)
            rhs = jnp.concatenate([h, m, h, m, l, h], axis=0).astype(bf16)
            upd = dot(lhs, rhs, 0, 0)
            for c in range(after, n):
                left[c] = jnp.where(done, 0.0, left[c]) - upd[8 * c:8 * c + 8, :]
    return up, inv

def chol_body(a_ref, out_ref, nblk, width):
    for k in range(nblk):
        r0 = k * NB
        rows = [a_ref[r0 + 8*b: r0 + 8*b + 8, r0:r0 + NB] for b in range(16)]
        up, inv = factor_block(rows)
        li = lax.broadcasted_iota(jnp.int32, (NB, NB), 1)
        si = lax.broadcasted_iota(jnp.int32, (NB, NB), 0)
        out_ref[r0:r0 + NB, r0:r0 + NB] = jnp.where(li >= si, jnp.concatenate(up, axis=0), 0.0)
        t = left_stack(jnp.concatenate(inv, axis=0), 1)
        if r0 > 0:
            out_ref[r0:r0 + NB, 0:r0] = jnp.zeros((NB, r0), f32)
        pieces = []
        lo = r0 + NB
        while lo < width:
            hi = min(lo + 2 * NB - lo % (2 * NB), width)
            p = dot(t, right_stack(a_ref[r0:r0 + NB, lo:hi], 0), 1, 0)
            out_ref[r0:r0 + NB, lo:hi] = p
            pieces.append((lo, hi, p))
            lo = hi
        if k + 1 < nblk:
            full = jnp.concatenate([left_stack(p.T, 1) for lo, hi, p in pieces if lo < nblk * NB], axis=0)
            for lo, hi, p in pieces:
                top, end = r0 + NB, min(hi, nblk * NB)
                a_ref[top:end, lo:hi] = a_ref[top:end, lo:hi] - dot(full[:end - top], right_stack(p, 0), 1, 0)


def exact(a, b):
    return lax.dot_general(
        a, b, (((1,), (0,)), ((), ())), precision=lax.Precision.HIGHEST, preferred_element_type=f32
    )


def blocks_of(nblk):
    return [(i, j) for i in range(nblk) for j in range(i, nblk)]


def fetch(pairs, sem):
    copies = [pltpu.make_async_copy(src, dst, sem.at[i]) for i, (src, dst) in enumerate(pairs)]
    for copy in copies:
        copy.start()
    return copies


def row_parts(rows):
    return [pl.ds(r, NB) for r in range(0, rows, NB)]


def arcs_kernel(design_hbm, weight_hbm, obs_hbm, arc_hbm, out_ref, design_ref, weight_ref, obs_ref, arc_ref, sem):
    rows, width = design_ref.shape
    pieces, each = out_ref.shape[:2]
    arcs = pieces * each // 2
    parts = row_parts(rows)
    copies = fetch(
        [(weight_hbm, weight_ref), (arc_hbm, arc_ref), (obs_hbm, obs_ref)]
        + [(design_hbm.at[p], design_ref.at[p]) for p in parts],
        sem,
    )
    for copy in copies[:3]:
        copy.wait()
    w = weight_ref[...]
    number = lax.broadcasted_iota(jnp.int32, (arcs, rows), 0)
    member = jnp.where(number == arc_ref[...], w * w, 0.0)
    total = jnp.sum(member, axis=1, keepdims=True)
    obs = jnp.sum(member * obs_ref[...], axis=1, keepdims=True)
    lane = lax.broadcasted_iota(jnp.int32, (arcs, NB), 1)
    tail = jnp.where(lane == 0, obs, jnp.where(lane == 1, total, 0.0))
    sums = None
    for n, p in enumerate(parts):
        copies[3 + n].wait()
        more = exact(member[:, n * NB:(n + 1) * NB], design_ref[p, :])
        sums = more if sums is None else sums + more
    sums = jnp.concatenate([sums, tail], axis=1)
    for n in range(pieces):
        at = n // 2 * each
        out_ref[n] = sums[at:at + each]


def half_kernel(mine, where_ref, tall_ref, flat_ref, p_ref, out_ref):
    width = flat_ref.shape[1]
    deep = flat_ref.shape[0] // 2
    nblk = width // NB
    order = blocks_of(nblk)
    half = len(order) // 2
    core = where_ref[0]

    def one(side):
        wanted = order[side * half:(side + 1) * half]
        for lo in range(0, nblk, 2):
            tops = sorted({i for i, j in wanted if j in (lo, lo + 1)})
            if not tops:
                continue
            cols = sorted({j for i, j in wanted if j in (lo, lo + 1)})
            c0, c1 = cols[0] * NB, cols[-1] * NB + NB
            r0, r1 = tops[0] * NB, tops[-1] * NB + NB
            g = dot(tall_ref[r0:r1, :], flat_ref[:, c0:c1], 1, 0)
            g = g + dot(tall_ref[r0:r1, :deep], flat_ref[deep:, c0:c1], 1, 0)
            for j in cols:
                for i in tops:
                    if (i, j) in wanted:
                        block = g[i * NB - r0:i * NB - r0 + NB, j * NB - c0:j * NB - c0 + NB]
                        at = wanted.index((i, j)) * NB
                        if i == j and i < 2:
                            corner = [p_ref[0:1, r * 64:(r + 1) * 64] for r in range(i * nblk, (i + 1) * nblk)]
                            corner = jnp.concatenate(corner, axis=0)
                            last = jnp.concatenate([corner, block[NB - 8:, 64:]], axis=1)
                            block = jnp.concatenate([block[:NB - 8], last], axis=0)
                        out_ref[at:at + NB, :] = block

    pl.when(core == (0 if mine else 1))(functools.partial(one, 0))
    pl.when(core == (1 if mine else 0))(functools.partial(one, 1))


def first_kernel(
    where_ref, design_ref, weight_ref, obs_ref, prior_ref, prhs_ref, after_ref, out_ref, tall_ref, flat_ref, p_ref
):
    rows, width = design_ref.shape
    prows = prior_ref.shape[0]
    deep = tall_ref.shape[1] // 2
    include = where_ref[1].astype(f32)
    w = weight_ref[...]
    wobs = jnp.broadcast_to(w * w * obs_ref[...], (8, rows))

    def place(r, z):
        for c in range(0, width, NB):
            h = z[:, c:c + NB].astype(bf16)
            m = (z[:, c:c + NB] - h.astype(f32)).astype(bf16)
            flat_ref[r:r + NB, c:c + NB] = m
            flat_ref[deep + r:deep + r + NB, c:c + NB] = h
            turned = z[:, c:c + NB].T
            h = turned.astype(bf16)
            tall_ref[c:c + NB, r:r + NB] = h
            tall_ref[c:c + NB, deep + r:deep + r + NB] = (turned - h.astype(f32)).astype(bf16)

    for r in range(0, rows, NB):
        column = jnp.broadcast_to(w[:, r:r + NB], (NB, NB)).T
        place(r, design_ref[r:r + NB, :] * jnp.concatenate([column] * (width // NB), axis=1))
    prior = prior_ref[...] * include
    place(rows, jnp.concatenate([prior, jnp.zeros((NB - prows, width), f32)], axis=0))
    p_ref[...] = exact(wobs, design_ref[...]) + exact(jnp.broadcast_to(prhs_ref[...], (8, prows)), prior)
    half_kernel(False, where_ref, tall_ref, flat_ref, p_ref, out_ref)


def pair_kernel(where_ref, mine_ref, got_ref, arcs_ref, out_ref):
    width = arcs_ref.shape[2] - NB
    nblk = width // NB
    order = blocks_of(nblk)
    half = len(order) // 2
    core = where_ref[0]
    s = arcs_ref[0]
    for r in range(1, arcs_ref.shape[0]):
        s = s + arcs_ref[r]
    s = jnp.concatenate([s, jnp.zeros((8 - s.shape[0], s.shape[1]), f32)], axis=0)
    total = s[:, width + 1:width + 2] + bias_prior
    b = s * lax.rsqrt(jnp.broadcast_to(total, s.shape))
    obs = b[:, width:width + 1]
    p = jnp.sum(b[:, :width] * obs, axis=0, keepdims=True)
    h = b.astype(bf16).astype(f32)
    m = (b - h).astype(bf16).astype(f32)
    l = b - h - m
    lhs = jnp.concatenate([h, h, m, m, h, l], axis=0).astype(bf16)
    rhs = jnp.concatenate([h, m, h, m, l, h], axis=0).astype(bf16)

    def one(side):
        for t in range(half):
            i, j = order[side * half + t]
            part = dot(lhs[:, i * NB:(i + 1) * NB], rhs[:, j * NB:(j + 1) * NB], 0, 0)
            if i == j and i < 2:
                mine_row = [
                    jnp.concatenate([p[:, r * 64:(r + 1) * 64], part[NB - 8 + r % nblk:NB - 8 + r % nblk + 1, 64:]], axis=1)
                    for r in range(i * nblk, (i + 1) * nblk)
                ]
                part = jnp.concatenate([part[:NB - 8]] + mine_row, axis=0)
            out_ref[t * NB:(t + 1) * NB, :] = mine_ref[t * NB:(t + 1) * NB, :] + got_ref[t * NB:(t + 1) * NB, :] - part

    pl.when(core == 0)(functools.partial(one, 0))
    pl.when(core == 1)(functools.partial(one, 1))


def factor_kernel(where_ref, mine_ref, other_ref, out_ref, rhs_ref, a_ref, u_ref):
    n = u_ref.shape[0]
    nblk = n // NB
    order = blocks_of(nblk)
    half = len(order) // 2
    core = where_ref[0]
    first = core == 0
    for t, (i, j) in enumerate(order):
        rows = pl.ds((t % half) * NB, NB)
        a, b = (mine_ref, other_ref) if t < half else (other_ref, mine_ref)
        a_ref[i * NB:(i + 1) * NB, j * NB:(j + 1) * NB] = jnp.where(first, a[rows, :], b[rows, :])
    lane = lax.broadcasted_iota(jnp.int32, (NB, NB), 1)
    for k in range(nblk):
        d = (2 * k // nblk) * NB
        r = d + NB - 8 + (2 * k) % nblk
        line = jnp.concatenate([a_ref[r:r + 1, d:d + 64], a_ref[r + 1:r + 2, d:d + 64]], axis=1)
        a_ref[k * NB:(k + 1) * NB, n:] = jnp.where(lane == 0, jnp.broadcast_to(line, (NB, NB)).T, 0.0)
    chol_body(a_ref, u_ref, nblk, n + NB)
    share = out_ref.shape[0]
    mine = pl.ds(pl.multiple_of(where_ref[1] * share, share), share)
    out_ref[...] = u_ref[mine, :n]
    rhs_ref[...] = u_ref[mine, n:].T[0:1, :]


def call(kernel, name, where, args, outs, scratch, grant, far=False, cost=None):
    return pl.pallas_call(
        kernel,
        out_shape=outs,
        in_specs=([SMEM] if where is not None else []) + [FAR if far else VMEM] * len(args),
        out_specs=jax.tree.map(lambda _: VMEM, outs),
        scratch_shapes=scratch,
        compiler_params=pltpu.CompilerParams(vmem_limit_bytes=grant * 2**20),
        cost_estimate=cost,
        name=name,
    )(*(() if where is None else (where,)), *args)


def like(*shape):
    return jax.ShapeDtypeStruct(shape, f32)


def on_device(design, observed, row_weight, arc_of_row, prior_factor, prior_rhs):
    rows, width = design.shape
    prows = prior_factor.shape[0]
    nz, nc = lax.axis_size(("zh", "zl")), lax.axis_size("core")
    core, z = lax.axis_index("core"), lax.axis_index(("zh", "zl"))
    arcs = 2 * nz * nc
    nblk = width // NB
    half = len(blocks_of(nblk)) // 2 * NB
    include = (lax.axis_index(("x", "yh", "yl")) == 0).astype(jnp.int32)
    weight = row_weight.reshape(1, rows)
    obs = observed.reshape(1, rows)
    arc = arc_of_row.reshape(1, rows)
    nparts = rows // NB
    deep = rows + NB
    here = jnp.stack([core, include]).astype(jnp.int32)
    partial = call(
        arcs_kernel,
        "arcs",
        None,
        (design, weight, obs, arc),
        like(nz * nc, 2 * nc, width + NB),
        [
            pltpu.VMEM((rows, width), f32),
            pltpu.VMEM((1, rows), f32),
            pltpu.VMEM((1, rows), f32),
            pltpu.VMEM((1, rows), jnp.int32),
            pltpu.SemaphoreType.DMA((3 + nparts,)),
        ],
        56,
        far=True,
    )
    owned = lax.all_to_all(partial, ("zh", "zl", "core"), 0, 0, tiled=True)
    work = pl.CostEstimate(flops=2 * 10**11, bytes_accessed=10**7, transcendentals=0)
    send, tall, flat, p = call(
        first_kernel,
        "first",
        here,
        (design, weight, obs, prior_factor, prior_rhs.reshape(1, prows), partial),
        (
            like(half, NB),
            pltpu.VMEM((width, 2 * deep), bf16),
            pltpu.VMEM((2 * deep, width), bf16),
            pltpu.VMEM((8, width), f32),
        ),
        [],
        20,
        cost=work,
    )
    keep = call(
        functools.partial(half_kernel, True), "keep", here, (tall, flat, p), pltpu.VMEM((half, NB), f32), [], 20, cost=work
    )
    swap = [(i, 1 - i) for i in range(nc)]
    got = lax.ppermute(send, "core", swap)
    where = jnp.stack([core, z * nc + core]).astype(jnp.int32)
    v = call(
        pair_kernel, "pair", where, (keep, got, owned), like(half, NB), [], 32
    )
    block, blocks = ("x", "yl", "zl"), ("yh", "zh")
    nb, nbs = lax.axis_size(block), lax.axis_size(blocks)
    v = lax.all_to_all(v.reshape(nb, half // nb, NB), block, 0, 0, tiled=True).sum(0)
    v = lax.all_to_all(v.reshape(nbs, 1, v.size // nbs), blocks, 0, 0, tiled=True).sum(0)
    v = lax.all_to_all(jnp.broadcast_to(v, (nbs, *v.shape)), blocks, 0, 0, tiled=True)
    v = v.reshape(half // nb, NB)
    v = lax.all_to_all(jnp.broadcast_to(v, (nb, *v.shape)), block, 0, 0, tiled=True)
    v = v.reshape(half, NB)
    other = lax.ppermute(v, "core", swap)
    factor, rhs = call(
        factor_kernel,
        "factor",
        where,
        (v, other),
        (like(prows, width), like(1, prows)),
        [pltpu.VMEM((width, width + NB), f32), pltpu.VMEM((width, width + NB), f32)],
        32,
    )
    return factor, rhs.reshape(prows)


def solution(mesh):
    fine = Mesh(mesh.devices.reshape(4, 4, 2, 4, 2, 2), ("x", "yh", "yl", "zh", "zl", "core"))
    dev = ("zh", "zl", "core")
    every = ("x", "yh", "yl") + dev
    placed = (P(every, None), P(every), P(every), P(every, None), P(dev, None), P(dev))
    return jax.shard_map(
        on_device,
        mesh=fine,
        in_specs=placed,
        out_specs=(P(dev, None), P(dev)),
        check_vma=False,
    )
```

```python
import functools

import jax
import jax.numpy as jnp
from jax import lax
from jax.experimental import pallas as pl
from jax.experimental.pallas import tpu as pltpu
from jax.sharding import Mesh
from jax.sharding import PartitionSpec as P

f32 = jnp.float32
bf16 = jnp.bfloat16
NB = 128
bias_prior = 1.0
VMEM = pl.BlockSpec(memory_space=pltpu.VMEM)
FAR = pl.BlockSpec(memory_space=pltpu.HBM)
SMEM = pl.BlockSpec(memory_space=pltpu.SMEM)


def spread(x, i):
    return jnp.broadcast_to(x[i:i+1, :], (8, x.shape[1]))

def across(x, lane):
    return jnp.broadcast_to(x[:, lane:lane+1], (8, 128))

def split(x):
    hi = x.astype(bf16)
    rest = x - hi.astype(f32)
    mid = rest.astype(bf16)
    return hi, mid, (rest - mid.astype(f32)).astype(bf16)

def left_stack(x, axis):
    h, m, l = split(x)
    return jnp.concatenate([h, h, m, m, h, l], axis=axis)

def right_stack(x, axis):
    h, m, l = split(x)
    return jnp.concatenate([h, m, h, m, l, h], axis=axis)

def dot(a, b, ca, cb):
    return lax.dot_general(a, b, (((ca,), (cb,)), ((), ())), preferred_element_type=f32)

def factor_block(rows, tall=2, ahead=2):
    sub = lax.broadcasted_iota(jnp.int32, (8, 128), 0)
    lane = lax.broadcasted_iota(jnp.int32, (8, 128), 1)
    n = 16
    left = list(rows)
    up, inv = [], []
    for b in range(0, n, tall):
        own = list(range(b, b + tall))
        near = list(range(b + tall, min(b + tall + ahead, n)))
        steps = 8 * tall
        col = [{c: across(left[c], 8 * b + j) for c in own[j // 8:] + near} for j in range(steps)]
        x = {c: left[c] for c in own}
        y = {c: jnp.where(lane == sub + 8 * c, 1.0, 0.0) for c in own}
        diag = {c: jnp.ones((8, 128), f32) for c in own}
        mults = []
        for j in range(steps):
            home = own[j // 8]
            q = 1.0 / spread(col[j][home], j % 8)
            diag[home] = jnp.where(sub == j % 8, q, diag[home])
            scaled = {c: col[j][c] * q for c in col[j]}
            for k in range(j + 1, steps):
                kh = own[k // 8]
                head = spread(col[j][kh], k % 8)
                for c in col[k]:
                    col[k][c] = col[k][c] - scaled[c] * head
            sx, sy = spread(x[home], j % 8), spread(y[home], j % 8)
            for c in own[j // 8:]:
                m = jnp.where(sub > j % 8, scaled[c], 0.0) if c == home else scaled[c]
                x[c] = x[c] - m * sx
                y[c] = y[c] - m * sy
            mults.append(scaled)
        done = (lane >= 8 * b) & (lane < 8 * (b + tall))
        z = {c: jnp.where(done, y[c], x[c]) for c in own}
        if near:
            lines = [spread(z[own[j // 8]], j % 8) for j in range(steps)]
        for c in near:
            dx = [mults[j][c] * lines[j] for j in range(steps)]
            while len(dx) > 1:
                dx = [dx[i] + dx[i + 1] for i in range(0, len(dx), 2)]
            left[c] = jnp.where(done, 0.0, left[c]) - dx[0]
        for c in own:
            r = jnp.sqrt(diag[c])
            up.append(x[c] * r)
            z[c] = z[c] * r
            inv.append(jnp.where(lane < 8 * (b + tall), z[c], 0.0))
        after = b + tall + ahead
        if after < n:
            w = jnp.concatenate([z[c] for c in own], axis=0)
            h = w.astype(bf16).astype(f32)
            m = (w - h).astype(bf16).astype(f32)
            l = w - h - m
            lhs = jnp.concatenate([h, h, m, m, h, l], axis=0).astype(bf16)
            rhs = jnp.concatenate([h, m, h, m, l, h], axis=0).astype(bf16)
            upd = dot(lhs, rhs, 0, 0)
            for c in range(after, n):
                left[c] = jnp.where(done, 0.0, left[c]) - upd[8 * c:8 * c + 8, :]
    return up, inv

def chol_body(a_ref, out_ref, nblk, width):
    for k in range(nblk):
        r0 = k * NB
        rows = [a_ref[r0 + 8*b: r0 + 8*b + 8, r0:r0 + NB] for b in range(16)]
        up, inv = factor_block(rows)
        li = lax.broadcasted_iota(jnp.int32, (NB, NB), 1)
        si = lax.broadcasted_iota(jnp.int32, (NB, NB), 0)
        out_ref[r0:r0 + NB, r0:r0 + NB] = jnp.where(li >= si, jnp.concatenate(up, axis=0), 0.0)
        t = left_stack(jnp.concatenate(inv, axis=0), 1)
        if r0 > 0:
            out_ref[r0:r0 + NB, 0:r0] = jnp.zeros((NB, r0), f32)
        pieces = []
        lo = r0 + NB
        while lo < width:
            hi = min(lo + 2 * NB - lo % (2 * NB), width)
            p = dot(t, right_stack(a_ref[r0:r0 + NB, lo:hi], 0), 1, 0)
            out_ref[r0:r0 + NB, lo:hi] = p
            pieces.append((lo, hi, p))
            lo = hi
        if k + 1 < nblk:
            full = jnp.concatenate([left_stack(p.T, 1) for lo, hi, p in pieces if lo < nblk * NB], axis=0)
            for lo, hi, p in pieces:
                top, end = r0 + NB, min(hi, nblk * NB)
                a_ref[top:end, lo:hi] = a_ref[top:end, lo:hi] - dot(full[:end - top], right_stack(p, 0), 1, 0)


def exact(a, b):
    return lax.dot_general(
        a, b, (((1,), (0,)), ((), ())), precision=lax.Precision.HIGHEST, preferred_element_type=f32
    )


def blocks_of(nblk):
    return [(i, j) for i in range(nblk) for j in range(i, nblk)]


def fetch(pairs, sem):
    copies = [pltpu.make_async_copy(src, dst, sem.at[i]) for i, (src, dst) in enumerate(pairs)]
    for copy in copies:
        copy.start()
    return copies


def row_parts(rows):
    return [pl.ds(r, NB) for r in range(0, rows, NB)]


def arcs_kernel(design_hbm, weight_hbm, obs_hbm, arc_hbm, out_ref, done_ref, design_ref, weight_ref, obs_ref, arc_ref, sem):
    rows, width = design_ref.shape
    pieces, each = out_ref.shape[:2]
    arcs = pieces * each // 2
    parts = row_parts(rows)
    copies = fetch(
        [(weight_hbm, weight_ref), (arc_hbm, arc_ref), (obs_hbm, obs_ref)]
        + [(design_hbm.at[p], design_ref.at[p]) for p in parts],
        sem,
    )
    for copy in copies[:3]:
        copy.wait()
    done_ref[...] = jnp.zeros_like(done_ref)
    w = weight_ref[...]
    number = lax.broadcasted_iota(jnp.int32, (arcs, rows), 0)
    member = jnp.where(number == arc_ref[...], w * w, 0.0)
    total = jnp.sum(member, axis=1, keepdims=True)
    obs = jnp.sum(member * obs_ref[...], axis=1, keepdims=True)
    lane = lax.broadcasted_iota(jnp.int32, (arcs, NB), 1)
    tail = jnp.where(lane == 0, obs, jnp.where(lane == 1, total, 0.0))
    sums = None
    for n, p in enumerate(parts):
        copies[3 + n].wait()
        more = exact(member[:, n * NB:(n + 1) * NB], design_ref[p, :])
        sums = more if sums is None else sums + more
    sums = jnp.concatenate([sums, tail], axis=1)
    for n in range(pieces):
        at = n // 2 * each
        out_ref[n] = sums[at:at + each]


def half_kernel(mine, where_ref, tall_ref, flat_ref, p_ref, out_ref):
    width = flat_ref.shape[1]
    deep = flat_ref.shape[0] // 2
    nblk = width // NB
    order = blocks_of(nblk)
    half = len(order) // 2
    core = where_ref[0]

    def one(side):
        wanted = order[side * half:(side + 1) * half]
        for lo in range(0, nblk, 2):
            tops = sorted({i for i, j in wanted if j in (lo, lo + 1)})
            if not tops:
                continue
            cols = sorted({j for i, j in wanted if j in (lo, lo + 1)})
            c0, c1 = cols[0] * NB, cols[-1] * NB + NB
            r0, r1 = tops[0] * NB, tops[-1] * NB + NB
            g = dot(tall_ref[r0:r1, :], flat_ref[:, c0:c1], 1, 0)
            g = g + dot(tall_ref[r0:r1, :deep], flat_ref[deep:, c0:c1], 1, 0)
            for j in cols:
                for i in tops:
                    if (i, j) in wanted:
                        block = g[i * NB - r0:i * NB - r0 + NB, j * NB - c0:j * NB - c0 + NB]
                        at = wanted.index((i, j)) * NB
                        if i == j and i < 2:
                            corner = [p_ref[0:1, r * 64:(r + 1) * 64] for r in range(i * nblk, (i + 1) * nblk)]
                            corner = jnp.concatenate(corner, axis=0)
                            last = jnp.concatenate([corner, block[NB - 8:, 64:]], axis=1)
                            block = jnp.concatenate([block[:NB - 8], last], axis=0)
                        out_ref[at:at + NB, :] = block

    pl.when(core == (0 if mine else 1))(functools.partial(one, 0))
    pl.when(core == (1 if mine else 0))(functools.partial(one, 1))


def first_kernel(
    where_ref, design_ref, weight_ref, obs_ref, prior_ref, prhs_ref, after_ref, out_ref, tall_ref, flat_ref, p_ref
):
    rows, width = design_ref.shape
    prows = prior_ref.shape[0]
    deep = tall_ref.shape[1] // 2
    include = where_ref[1].astype(f32)
    w = weight_ref[...]
    wobs = jnp.broadcast_to(w * w * obs_ref[...], (8, rows))

    def place(r, z):
        for c in range(0, width, NB):
            h = z[:, c:c + NB].astype(bf16)
            m = (z[:, c:c + NB] - h.astype(f32)).astype(bf16)
            flat_ref[r:r + NB, c:c + NB] = m
            flat_ref[deep + r:deep + r + NB, c:c + NB] = h
            turned = z[:, c:c + NB].T
            h = turned.astype(bf16)
            tall_ref[c:c + NB, r:r + NB] = h
            tall_ref[c:c + NB, deep + r:deep + r + NB] = (turned - h.astype(f32)).astype(bf16)

    for r in range(0, rows, NB):
        column = jnp.broadcast_to(w[:, r:r + NB], (NB, NB)).T
        place(r, design_ref[r:r + NB, :] * jnp.concatenate([column] * (width // NB), axis=1))
    prior = prior_ref[...] * include
    place(rows, jnp.concatenate([prior, jnp.zeros((NB - prows, width), f32)], axis=0))
    p_ref[...] = exact(wobs, design_ref[...]) + exact(jnp.broadcast_to(prhs_ref[...], (8, prows)), prior)
    half_kernel(False, where_ref, tall_ref, flat_ref, p_ref, out_ref)


def pair_kernel(where_ref, mine_ref, got_ref, arcs_ref, out_ref):
    width = arcs_ref.shape[2] - NB
    nblk = width // NB
    order = blocks_of(nblk)
    half = len(order) // 2
    core = where_ref[0]
    s = arcs_ref[0]
    for r in range(1, arcs_ref.shape[0]):
        s = s + arcs_ref[r]
    s = jnp.concatenate([s, jnp.zeros((8 - s.shape[0], s.shape[1]), f32)], axis=0)
    total = s[:, width + 1:width + 2] + bias_prior
    b = s * lax.rsqrt(jnp.broadcast_to(total, s.shape))
    obs = b[:, width:width + 1]
    p = jnp.sum(b[:, :width] * obs, axis=0, keepdims=True)
    h = b.astype(bf16).astype(f32)
    m = (b - h).astype(bf16).astype(f32)
    l = b - h - m
    lhs = jnp.concatenate([h, h, m, m, h, l], axis=0).astype(bf16)
    rhs = jnp.concatenate([h, m, h, m, l, h], axis=0).astype(bf16)

    def one(side):
        for t in range(half):
            i, j = order[side * half + t]
            part = dot(lhs[:, i * NB:(i + 1) * NB], rhs[:, j * NB:(j + 1) * NB], 0, 0)
            if i == j and i < 2:
                mine_row = [
                    jnp.concatenate([p[:, r * 64:(r + 1) * 64], part[NB - 8 + r % nblk:NB - 8 + r % nblk + 1, 64:]], axis=1)
                    for r in range(i * nblk, (i + 1) * nblk)
                ]
                part = jnp.concatenate([part[:NB - 8]] + mine_row, axis=0)
            out_ref[t * NB:(t + 1) * NB, :] = mine_ref[t * NB:(t + 1) * NB, :] + got_ref[t * NB:(t + 1) * NB, :] - part

    pl.when(core == 0)(functools.partial(one, 0))
    pl.when(core == 1)(functools.partial(one, 1))


def factor_kernel(where_ref, mine_ref, other_ref, out_ref, rhs_ref, a_ref, u_ref):
    n = u_ref.shape[0]
    nblk = n // NB
    order = blocks_of(nblk)
    half = len(order) // 2
    core = where_ref[0]
    first = core == 0
    for t, (i, j) in enumerate(order):
        rows = pl.ds((t % half) * NB, NB)
        a, b = (mine_ref, other_ref) if t < half else (other_ref, mine_ref)
        a_ref[i * NB:(i + 1) * NB, j * NB:(j + 1) * NB] = jnp.where(first, a[rows, :], b[rows, :])
    lane = lax.broadcasted_iota(jnp.int32, (NB, NB), 1)
    for k in range(nblk):
        d = (2 * k // nblk) * NB
        r = d + NB - 8 + (2 * k) % nblk
        line = jnp.concatenate([a_ref[r:r + 1, d:d + 64], a_ref[r + 1:r + 2, d:d + 64]], axis=1)
        a_ref[k * NB:(k + 1) * NB, n:] = jnp.where(lane == 0, jnp.broadcast_to(line, (NB, NB)).T, 0.0)
    chol_body(a_ref, u_ref, nblk, n + NB)
    share = out_ref.shape[0]
    mine = pl.ds(pl.multiple_of(where_ref[1] * share, share), share)
    out_ref[...] = u_ref[mine, :n]
    rhs_ref[...] = u_ref[mine, n:].T[0:1, :]


def call(kernel, name, where, args, outs, scratch, grant, far=False, cost=None):
    return pl.pallas_call(
        kernel,
        out_shape=outs,
        in_specs=([SMEM] if where is not None else []) + [FAR if far else VMEM] * len(args),
        out_specs=jax.tree.map(lambda _: VMEM, outs),
        scratch_shapes=scratch,
        compiler_params=pltpu.CompilerParams(vmem_limit_bytes=grant * 2**20),
        cost_estimate=cost,
        name=name,
    )(*(() if where is None else (where,)), *args)


def like(*shape):
    return jax.ShapeDtypeStruct(shape, f32)


def on_device(design, observed, row_weight, arc_of_row, prior_factor, prior_rhs):
    rows, width = design.shape
    prows = prior_factor.shape[0]
    nz, nc = lax.axis_size(("zh", "zl")), lax.axis_size("core")
    core, z = lax.axis_index("core"), lax.axis_index(("zh", "zl"))
    arcs = 2 * nz * nc
    nblk = width // NB
    half = len(blocks_of(nblk)) // 2 * NB
    include = (lax.axis_index(("x", "yh", "yl")) == 0).astype(jnp.int32)
    weight = row_weight.reshape(1, rows)
    obs = observed.reshape(1, rows)
    arc = arc_of_row.reshape(1, rows)
    nparts = rows // NB
    deep = rows + NB
    here = jnp.stack([core, include]).astype(jnp.int32)
    partial, done = call(
        arcs_kernel,
        "arcs",
        None,
        (design, weight, obs, arc),
        (like(nz * nc, 2 * nc, width + NB), like(8, NB)),
        [
            pltpu.VMEM((rows, width), f32),
            pltpu.VMEM((1, rows), f32),
            pltpu.VMEM((1, rows), f32),
            pltpu.VMEM((1, rows), jnp.int32),
            pltpu.SemaphoreType.DMA((3 + nparts,)),
        ],
        56,
        far=True,
    )
    owned = lax.all_to_all(partial, ("zh", "zl", "core"), 0, 0, tiled=True)
    work = pl.CostEstimate(flops=2 * 10**11, bytes_accessed=10**7, transcendentals=0)
    send, tall, flat, p = call(
        first_kernel,
        "first",
        here,
        (design, weight, obs, prior_factor, prior_rhs.reshape(1, prows), done),
        (
            like(half, NB),
            pltpu.VMEM((width, 2 * deep), bf16),
            pltpu.VMEM((2 * deep, width), bf16),
            pltpu.VMEM((8, width), f32),
        ),
        [],
        20,
        cost=work,
    )
    keep = call(
        functools.partial(half_kernel, True), "keep", here, (tall, flat, p), pltpu.VMEM((half, NB), f32), [], 20, cost=work
    )
    swap = [(i, 1 - i) for i in range(nc)]
    got = lax.ppermute(send, "core", swap)
    where = jnp.stack([core, z * nc + core]).astype(jnp.int32)
    v = call(
        pair_kernel, "pair", where, (keep, got, owned), like(half, NB), [], 32
    )
    block = ("x", "yl", "zl")
    nb, ny, nzh = (lax.axis_size(a) for a in (block, "yh", "zh"))
    v = lax.all_to_all(v.reshape(nb, half // nb, NB), block, 0, 0, tiled=True).sum(0)
    v = lax.all_to_all(v.reshape(ny, 1, v.size // ny), "yh", 0, 0, tiled=True).sum(0)
    v = lax.all_to_all(jnp.broadcast_to(v, (nzh, *v.shape)), "zh", 0, 0, tiled=True).sum(0)
    v = lax.all_to_all(jnp.broadcast_to(v, (ny, *v.shape)), "yh", 0, 0, tiled=True)
    v = v.reshape(half // nb, NB)
    v = lax.all_to_all(jnp.broadcast_to(v, (nb, *v.shape)), block, 0, 0, tiled=True)
    v = v.reshape(half, NB)
    other = lax.ppermute(v, "core", swap)
    factor, rhs = call(
        factor_kernel,
        "factor",
        where,
        (v, other),
        (like(prows, width), like(1, prows)),
        [pltpu.VMEM((width, width + NB), f32), pltpu.VMEM((width, width + NB), f32)],
        32,
    )
    return factor, rhs.reshape(prows)


def solution(mesh):
    fine = Mesh(mesh.devices.reshape(4, 4, 2, 4, 2, 2), ("x", "yh", "yl", "zh", "zl", "core"))
    dev = ("zh", "zl", "core")
    every = ("x", "yh", "yl") + dev
    placed = (P(every, None), P(every), P(every), P(every, None), P(dev, None), P(dev))
    return jax.shard_map(
        on_device,
        mesh=fine,
        in_specs=placed,
        out_specs=(P(dev, None), P(dev)),
        check_vma=False,
    )
```

```python
import functools

import jax
import jax.numpy as jnp
from jax import lax
from jax.experimental import pallas as pl
from jax.experimental.pallas import tpu as pltpu
from jax.sharding import Mesh
from jax.sharding import PartitionSpec as P

f32 = jnp.float32
bf16 = jnp.bfloat16
NB = 128
bias_prior = 1.0
VMEM = pl.BlockSpec(memory_space=pltpu.VMEM)
FAR = pl.BlockSpec(memory_space=pltpu.HBM)
SMEM = pl.BlockSpec(memory_space=pltpu.SMEM)


def spread(x, i):
    return jnp.broadcast_to(x[i:i+1, :], (8, x.shape[1]))

def across(x, lane):
    return jnp.broadcast_to(x[:, lane:lane+1], (8, 128))

def split(x):
    hi = x.astype(bf16)
    rest = x - hi.astype(f32)
    mid = rest.astype(bf16)
    return hi, mid, (rest - mid.astype(f32)).astype(bf16)

def left_stack(x, axis):
    h, m, l = split(x)
    return jnp.concatenate([h, h, m, m, h, l], axis=axis)

def right_stack(x, axis):
    h, m, l = split(x)
    return jnp.concatenate([h, m, h, m, l, h], axis=axis)

def dot(a, b, ca, cb):
    return lax.dot_general(a, b, (((ca,), (cb,)), ((), ())), preferred_element_type=f32)

def factor_block(rows, side=None, tall=2, ahead=2):
    sub = lax.broadcasted_iota(jnp.int32, (8, 128), 0)
    lane = lax.broadcasted_iota(jnp.int32, (8, 128), 1)
    n = 16
    left = list(rows)
    up, inv = [], []
    for b in range(0, n, tall):
        own = list(range(b, b + tall))
        near = list(range(b + tall, min(b + tall + ahead, n)))
        steps = 8 * tall
        col = [{c: across(left[c], 8 * b + j) for c in own[j // 8:] + near} for j in range(steps)]
        if side is not None:
            next(side, None)
        x = {c: left[c] for c in own}
        y = {c: jnp.where(lane == sub + 8 * c, 1.0, 0.0) for c in own}
        diag = {c: jnp.ones((8, 128), f32) for c in own}
        mults, heads, qs = [], {}, []
        for j in range(steps):
            home = own[j // 8]
            q = 1.0 / spread(col[j][home], j % 8)
            diag[home] = jnp.where(sub == j % 8, q, diag[home])
            scaled = {c: col[j][c] * q for c in own[j // 8:]}
            qs.append(q)
            for k in range(j + 1, steps):
                kh = own[k // 8]
                head = spread(col[j][kh], k % 8)
                heads[j, k] = head
                for c in own[k // 8:]:
                    col[k][c] = col[k][c] - scaled[c] * head
            sx, sy = spread(x[home], j % 8), spread(y[home], j % 8)
            for c in own[j // 8:]:
                m = jnp.where(sub > j % 8, scaled[c], 0.0) if c == home else scaled[c]
                x[c] = x[c] - m * sx
                y[c] = y[c] - m * sy
        for j in range(steps):
            mults.append({c: col[j][c] * qs[j] for c in near})
            for k in range(j + 1, steps):
                for c in near:
                    col[k][c] = col[k][c] - mults[j][c] * heads[j, k]
        done = (lane >= 8 * b) & (lane < 8 * (b + tall))
        z = {c: jnp.where(done, y[c], x[c]) for c in own}
        if near:
            lines = [spread(z[own[j // 8]], j % 8) for j in range(steps)]
        for c in near:
            dx = [mults[j][c] * lines[j] for j in range(steps)]
            while len(dx) > 1:
                dx = [dx[i] + dx[i + 1] for i in range(0, len(dx), 2)]
            left[c] = jnp.where(done, 0.0, left[c]) - dx[0]
        for c in own:
            r = jnp.sqrt(diag[c])
            up.append(x[c] * r)
            z[c] = z[c] * r
            inv.append(jnp.where(lane < 8 * (b + tall), z[c], 0.0))
        after = b + tall + ahead
        if after < n:
            w = jnp.concatenate([z[c] for c in own], axis=0)
            h = w.astype(bf16).astype(f32)
            m = (w - h).astype(bf16).astype(f32)
            l = w - h - m
            lhs = jnp.concatenate([h, h, m, m, h, l], axis=0).astype(bf16)
            rhs = jnp.concatenate([h, m, h, m, l, h], axis=0).astype(bf16)
            upd = dot(lhs, rhs, 0, 0)
            for c in range(after, n):
                left[c] = jnp.where(done, 0.0, left[c]) - upd[8 * c:8 * c + 8, :]
    return up, inv

def strips(lo, hi):
    spans = []
    while lo < hi:
        end = min(lo + 2 * NB - lo % (2 * NB), hi)
        spans.append((lo, end))
        lo = end
    return spans


def later_work(a_ref, out_ref, t, p, r0, n, width):
    top = r0 + NB
    turned = [left_stack(p.T, 1)]
    flat = right_stack(p, 0)
    pieces = []
    for lo, hi in strips(top + NB, width):
        q = dot(t, right_stack(a_ref[r0:top, lo:hi], 0), 1, 0)
        out_ref[r0:top, lo:hi] = q
        pieces.append((lo, hi, right_stack(q, 0)))
        if lo < n:
            turned.append(left_stack(q.T, 1))
        yield
    full = jnp.concatenate(turned, axis=0)
    for lo, hi, q in pieces:
        end = min(hi, n)
        a_ref[top:end, lo:hi] = a_ref[top:end, lo:hi] - dot(full[:end - top], q, 1, 0)
        yield


def chol_body(a_ref, out_ref, nblk, width):
    n = nblk * NB
    li = lax.broadcasted_iota(jnp.int32, (NB, NB), 1)
    si = lax.broadcasted_iota(jnp.int32, (NB, NB), 0)
    side = None
    for k in range(nblk):
        r0 = k * NB
        rows = [a_ref[r0 + 8 * b:r0 + 8 * b + 8, r0:r0 + NB] for b in range(16)]
        up, inv = factor_block(rows, side)
        if side is not None:
            for _ in side:
                pass
        out_ref[r0:r0 + NB, r0:r0 + NB] = jnp.where(li >= si, jnp.concatenate(up, axis=0), 0.0)
        if r0 > 0:
            out_ref[r0:r0 + NB, 0:r0] = jnp.zeros((NB, r0), f32)
        t = left_stack(jnp.concatenate(inv, axis=0), 1)
        top = r0 + NB
        p = dot(t, right_stack(a_ref[r0:top, top:top + NB], 0), 1, 0)
        out_ref[r0:top, top:top + NB] = p
        if k + 1 < nblk:
            a_ref[top:top + NB, top:top + NB] = a_ref[top:top + NB, top:top + NB] - dot(
                left_stack(p.T, 1), right_stack(p, 0), 1, 0
            )
            side = later_work(a_ref, out_ref, t, p, r0, n, width)


def exact(a, b):
    return lax.dot_general(
        a, b, (((1,), (0,)), ((), ())), precision=lax.Precision.HIGHEST, preferred_element_type=f32
    )


def blocks_of(nblk):
    return [(i, j) for i in range(nblk) for j in range(i, nblk)]


def fetch(pairs, sem):
    copies = [pltpu.make_async_copy(src, dst, sem.at[i]) for i, (src, dst) in enumerate(pairs)]
    for copy in copies:
        copy.start()
    return copies


def row_parts(rows):
    return [pl.ds(r, NB) for r in range(0, rows, NB)]


def arcs_kernel(design_hbm, weight_hbm, obs_hbm, arc_hbm, out_ref, done_ref, design_ref, weight_ref, obs_ref, arc_ref, sem):
    rows, width = design_ref.shape
    pieces, each = out_ref.shape[:2]
    arcs = pieces * each // 2
    parts = row_parts(rows)
    copies = fetch(
        [(weight_hbm, weight_ref), (arc_hbm, arc_ref), (obs_hbm, obs_ref)]
        + [(design_hbm.at[p], design_ref.at[p]) for p in parts],
        sem,
    )
    for copy in copies[:3]:
        copy.wait()
    done_ref[...] = jnp.zeros_like(done_ref)
    w = weight_ref[...]
    number = lax.broadcasted_iota(jnp.int32, (arcs, rows), 0)
    member = jnp.where(number == arc_ref[...], w * w, 0.0)
    total = jnp.sum(member, axis=1, keepdims=True)
    obs = jnp.sum(member * obs_ref[...], axis=1, keepdims=True)
    lane = lax.broadcasted_iota(jnp.int32, (arcs, NB), 1)
    tail = jnp.where(lane == 0, obs, jnp.where(lane == 1, total, 0.0))
    sums = None
    for n, p in enumerate(parts):
        copies[3 + n].wait()
        more = exact(member[:, n * NB:(n + 1) * NB], design_ref[p, :])
        sums = more if sums is None else sums + more
    sums = jnp.concatenate([sums, tail], axis=1)
    for n in range(pieces):
        at = n // 2 * each
        out_ref[n] = sums[at:at + each]


def half_kernel(mine, where_ref, tall_ref, flat_ref, p_ref, out_ref):
    width = flat_ref.shape[1]
    deep = flat_ref.shape[0] // 2
    nblk = width // NB
    order = blocks_of(nblk)
    half = len(order) // 2
    core = where_ref[0]

    def one(side):
        wanted = order[side * half:(side + 1) * half]
        for lo in range(0, nblk, 2):
            tops = sorted({i for i, j in wanted if j in (lo, lo + 1)})
            if not tops:
                continue
            cols = sorted({j for i, j in wanted if j in (lo, lo + 1)})
            c0, c1 = cols[0] * NB, cols[-1] * NB + NB
            r0, r1 = tops[0] * NB, tops[-1] * NB + NB
            g = dot(tall_ref[r0:r1, :], flat_ref[:, c0:c1], 1, 0)
            g = g + dot(tall_ref[r0:r1, :deep], flat_ref[deep:, c0:c1], 1, 0)
            for j in cols:
                for i in tops:
                    if (i, j) in wanted:
                        block = g[i * NB - r0:i * NB - r0 + NB, j * NB - c0:j * NB - c0 + NB]
                        at = wanted.index((i, j)) * NB
                        if i == j and i < 2:
                            corner = [p_ref[0:1, r * 64:(r + 1) * 64] for r in range(i * nblk, (i + 1) * nblk)]
                            corner = jnp.concatenate(corner, axis=0)
                            last = jnp.concatenate([corner, block[NB - 8:, 64:]], axis=1)
                            block = jnp.concatenate([block[:NB - 8], last], axis=0)
                        out_ref[at:at + NB, :] = block

    pl.when(core == (0 if mine else 1))(functools.partial(one, 0))
    pl.when(core == (1 if mine else 0))(functools.partial(one, 1))


def first_kernel(
    where_ref, design_ref, weight_ref, obs_ref, prior_ref, prhs_ref, after_ref, out_ref, tall_ref, flat_ref, p_ref
):
    rows, width = design_ref.shape
    prows = prior_ref.shape[0]
    deep = tall_ref.shape[1] // 2
    include = where_ref[1].astype(f32)
    w = weight_ref[...]
    wobs = jnp.broadcast_to(w * w * obs_ref[...], (8, rows))

    def place(r, z):
        for c in range(0, width, NB):
            h = z[:, c:c + NB].astype(bf16)
            m = (z[:, c:c + NB] - h.astype(f32)).astype(bf16)
            flat_ref[r:r + NB, c:c + NB] = m
            flat_ref[deep + r:deep + r + NB, c:c + NB] = h
            turned = z[:, c:c + NB].T
            h = turned.astype(bf16)
            tall_ref[c:c + NB, r:r + NB] = h
            tall_ref[c:c + NB, deep + r:deep + r + NB] = (turned - h.astype(f32)).astype(bf16)

    for r in range(0, rows, NB):
        column = jnp.broadcast_to(w[:, r:r + NB], (NB, NB)).T
        place(r, design_ref[r:r + NB, :] * jnp.concatenate([column] * (width // NB), axis=1))
    prior = prior_ref[...] * include
    place(rows, jnp.concatenate([prior, jnp.zeros((NB - prows, width), f32)], axis=0))
    p_ref[...] = exact(wobs, design_ref[...]) + exact(jnp.broadcast_to(prhs_ref[...], (8, prows)), prior)
    half_kernel(False, where_ref, tall_ref, flat_ref, p_ref, out_ref)


def pair_kernel(where_ref, mine_ref, got_ref, arcs_ref, out_ref):
    width = arcs_ref.shape[2] - NB
    nblk = width // NB
    order = blocks_of(nblk)
    half = len(order) // 2
    core = where_ref[0]
    s = arcs_ref[0]
    for r in range(1, arcs_ref.shape[0]):
        s = s + arcs_ref[r]
    s = jnp.concatenate([s, jnp.zeros((8 - s.shape[0], s.shape[1]), f32)], axis=0)
    total = s[:, width + 1:width + 2] + bias_prior
    b = s * lax.rsqrt(jnp.broadcast_to(total, s.shape))
    obs = b[:, width:width + 1]
    p = jnp.sum(b[:, :width] * obs, axis=0, keepdims=True)
    h = b.astype(bf16).astype(f32)
    m = (b - h).astype(bf16).astype(f32)
    l = b - h - m
    lhs = jnp.concatenate([h, h, m, m, h, l], axis=0).astype(bf16)
    rhs = jnp.concatenate([h, m, h, m, l, h], axis=0).astype(bf16)

    def one(side):
        for t in range(half):
            i, j = order[side * half + t]
            part = dot(lhs[:, i * NB:(i + 1) * NB], rhs[:, j * NB:(j + 1) * NB], 0, 0)
            if i == j and i < 2:
                mine_row = [
                    jnp.concatenate([p[:, r * 64:(r + 1) * 64], part[NB - 8 + r % nblk:NB - 8 + r % nblk + 1, 64:]], axis=1)
                    for r in range(i * nblk, (i + 1) * nblk)
                ]
                part = jnp.concatenate([part[:NB - 8]] + mine_row, axis=0)
            out_ref[t * NB:(t + 1) * NB, :] = mine_ref[t * NB:(t + 1) * NB, :] + got_ref[t * NB:(t + 1) * NB, :] - part

    pl.when(core == 0)(functools.partial(one, 0))
    pl.when(core == 1)(functools.partial(one, 1))


def factor_kernel(where_ref, mine_ref, other_ref, out_ref, rhs_ref, a_ref, u_ref):
    n = u_ref.shape[0]
    nblk = n // NB
    order = blocks_of(nblk)
    half = len(order) // 2
    core = where_ref[0]
    first = core == 0
    for t, (i, j) in enumerate(order):
        rows = pl.ds((t % half) * NB, NB)
        a, b = (mine_ref, other_ref) if t < half else (other_ref, mine_ref)
        a_ref[i * NB:(i + 1) * NB, j * NB:(j + 1) * NB] = jnp.where(first, a[rows, :], b[rows, :])
    lane = lax.broadcasted_iota(jnp.int32, (NB, NB), 1)
    for k in range(nblk):
        d = (2 * k // nblk) * NB
        r = d + NB - 8 + (2 * k) % nblk
        line = jnp.concatenate([a_ref[r:r + 1, d:d + 64], a_ref[r + 1:r + 2, d:d + 64]], axis=1)
        a_ref[k * NB:(k + 1) * NB, n:] = jnp.where(lane == 0, jnp.broadcast_to(line, (NB, NB)).T, 0.0)
    chol_body(a_ref, u_ref, nblk, n + NB)
    share = out_ref.shape[0]
    mine = pl.ds(pl.multiple_of(where_ref[1] * share, share), share)
    out_ref[...] = u_ref[mine, :n]
    rhs_ref[...] = u_ref[mine, n:].T[0:1, :]


def call(kernel, name, where, args, outs, scratch, grant, far=False, cost=None):
    return pl.pallas_call(
        kernel,
        out_shape=outs,
        in_specs=([SMEM] if where is not None else []) + [FAR if far else VMEM] * len(args),
        out_specs=jax.tree.map(lambda _: VMEM, outs),
        scratch_shapes=scratch,
        compiler_params=pltpu.CompilerParams(vmem_limit_bytes=grant * 2**20),
        cost_estimate=cost,
        name=name,
    )(*(() if where is None else (where,)), *args)


def like(*shape):
    return jax.ShapeDtypeStruct(shape, f32)


def on_device(design, observed, row_weight, arc_of_row, prior_factor, prior_rhs):
    rows, width = design.shape
    prows = prior_factor.shape[0]
    nz, nc = lax.axis_size(("zh", "zl")), lax.axis_size("core")
    core, z = lax.axis_index("core"), lax.axis_index(("zh", "zl"))
    arcs = 2 * nz * nc
    nblk = width // NB
    half = len(blocks_of(nblk)) // 2 * NB
    include = (lax.axis_index(("x", "yh", "yl")) == 0).astype(jnp.int32)
    weight = row_weight.reshape(1, rows)
    obs = observed.reshape(1, rows)
    arc = arc_of_row.reshape(1, rows)
    nparts = rows // NB
    deep = rows + NB
    here = jnp.stack([core, include]).astype(jnp.int32)
    partial, done = call(
        arcs_kernel,
        "arcs",
        None,
        (design, weight, obs, arc),
        (like(nz * nc, 2 * nc, width + NB), like(8, NB)),
        [
            pltpu.VMEM((rows, width), f32),
            pltpu.VMEM((1, rows), f32),
            pltpu.VMEM((1, rows), f32),
            pltpu.VMEM((1, rows), jnp.int32),
            pltpu.SemaphoreType.DMA((3 + nparts,)),
        ],
        56,
        far=True,
    )
    owned = lax.all_to_all(partial, ("zh", "zl", "core"), 0, 0, tiled=True)
    work = pl.CostEstimate(flops=2 * 10**11, bytes_accessed=10**7, transcendentals=0)
    send, tall, flat, p = call(
        first_kernel,
        "first",
        here,
        (design, weight, obs, prior_factor, prior_rhs.reshape(1, prows), done),
        (
            like(half, NB),
            pltpu.VMEM((width, 2 * deep), bf16),
            pltpu.VMEM((2 * deep, width), bf16),
            pltpu.VMEM((8, width), f32),
        ),
        [],
        20,
        cost=work,
    )
    keep = call(
        functools.partial(half_kernel, True), "keep", here, (tall, flat, p), pltpu.VMEM((half, NB), f32), [], 20, cost=work
    )
    swap = [(i, 1 - i) for i in range(nc)]
    got = lax.ppermute(send, "core", swap)
    where = jnp.stack([core, z * nc + core]).astype(jnp.int32)
    v = call(
        pair_kernel, "pair", where, (keep, got, owned), like(half, NB), [], 32
    )
    block = ("x", "yl", "zl")
    nb, ny, nzh = (lax.axis_size(a) for a in (block, "yh", "zh"))
    v = lax.all_to_all(v.reshape(nb, half // nb, NB), block, 0, 0, tiled=True).sum(0)
    v = lax.all_to_all(v.reshape(ny, 1, v.size // ny), "yh", 0, 0, tiled=True).sum(0)
    v = lax.all_to_all(jnp.broadcast_to(v, (ny * nzh, *v.shape)), ("yh", "zh"), 0, 0, tiled=True)
    v = v.reshape(ny, nzh, 1, v.shape[-1]).sum(1).reshape(half // nb, NB)
    v = lax.all_to_all(jnp.broadcast_to(v, (nb, *v.shape)), block, 0, 0, tiled=True)
    v = v.reshape(half, NB)
    other = lax.ppermute(v, "core", swap)
    factor, rhs = call(
        factor_kernel,
        "factor",
        where,
        (v, other),
        (like(prows, width), like(1, prows)),
        [pltpu.VMEM((width, width + NB), f32), pltpu.VMEM((width, width + NB), f32)],
        32,
    )
    return factor, rhs.reshape(prows)


def solution(mesh):
    fine = Mesh(mesh.devices.reshape(4, 4, 2, 4, 2, 2), ("x", "yh", "yl", "zh", "zl", "core"))
    dev = ("zh", "zl", "core")
    every = ("x", "yh", "yl") + dev
    placed = (P(every, None), P(every), P(every), P(every, None), P(dev, None), P(dev))
    return jax.shard_map(
        on_device,
        mesh=fine,
        in_specs=placed,
        out_specs=(P(dev, None), P(dev)),
        check_vma=False,
    )
```

```python
import functools

import jax
import jax.numpy as jnp
from jax import lax
from jax.experimental import pallas as pl
from jax.experimental.pallas import tpu as pltpu
from jax.sharding import Mesh
from jax.sharding import PartitionSpec as P

f32 = jnp.float32
bf16 = jnp.bfloat16
NB = 128
bias_prior = 1.0
VMEM = pl.BlockSpec(memory_space=pltpu.VMEM)
FAR = pl.BlockSpec(memory_space=pltpu.HBM)
SMEM = pl.BlockSpec(memory_space=pltpu.SMEM)


def spread(x, i):
    return jnp.broadcast_to(x[i:i+1, :], (8, x.shape[1]))

def across(x, lane):
    return jnp.broadcast_to(x[:, lane:lane+1], (8, 128))

def split(x):
    hi = x.astype(bf16)
    rest = x - hi.astype(f32)
    mid = rest.astype(bf16)
    return hi, mid, (rest - mid.astype(f32)).astype(bf16)

def left_stack(x, axis):
    h, m, l = split(x)
    return jnp.concatenate([h, h, m, m, h, l], axis=axis)

def right_stack(x, axis):
    h, m, l = split(x)
    return jnp.concatenate([h, m, h, m, l, h], axis=axis)

def dot(a, b, ca, cb):
    return lax.dot_general(a, b, (((ca,), (cb,)), ((), ())), preferred_element_type=f32)

def factor_block(rows, side=None, tall=2, ahead=2):
    sub = lax.broadcasted_iota(jnp.int32, (8, 128), 0)
    lane = lax.broadcasted_iota(jnp.int32, (8, 128), 1)
    n = 16
    left = list(rows)
    up, inv = [], []
    for b in range(0, n, tall):
        own = list(range(b, b + tall))
        near = list(range(b + tall, min(b + tall + ahead, n)))
        steps = 8 * tall
        col = [{c: across(left[c], 8 * b + j) for c in own[j // 8:] + near} for j in range(steps)]
        if side is not None:
            next(side, None)
        x = {c: left[c] for c in own}
        y = {c: jnp.where(lane == sub + 8 * c, 1.0, 0.0) for c in own}
        diag = {c: jnp.ones((8, 128), f32) for c in own}
        mults, heads, qs = [], {}, []
        for j in range(steps):
            home = own[j // 8]
            q = 1.0 / spread(col[j][home], j % 8)
            diag[home] = jnp.where(sub == j % 8, q, diag[home])
            scaled = {c: col[j][c] * q for c in own[j // 8:]}
            qs.append(q)
            for k in range(j + 1, steps):
                kh = own[k // 8]
                head = spread(col[j][kh], k % 8)
                heads[j, k] = head
                for c in own[k // 8:]:
                    col[k][c] = col[k][c] - scaled[c] * head
            sx, sy = spread(x[home], j % 8), spread(y[home], j % 8)
            for c in own[j // 8:]:
                m = jnp.where(sub > j % 8, scaled[c], 0.0) if c == home else scaled[c]
                x[c] = x[c] - m * sx
                y[c] = y[c] - m * sy
        for j in range(steps):
            mults.append({c: col[j][c] * qs[j] for c in near})
            for k in range(j + 1, steps):
                for c in near:
                    col[k][c] = col[k][c] - mults[j][c] * heads[j, k]
        done = (lane >= 8 * b) & (lane < 8 * (b + tall))
        z = {c: jnp.where(done, y[c], x[c]) for c in own}
        if near:
            lines = [spread(z[own[j // 8]], j % 8) for j in range(steps)]
        for c in near:
            dx = [mults[j][c] * lines[j] for j in range(steps)]
            while len(dx) > 1:
                dx = [dx[i] + dx[i + 1] for i in range(0, len(dx), 2)]
            left[c] = jnp.where(done, 0.0, left[c]) - dx[0]
        for c in own:
            r = jnp.sqrt(diag[c])
            up.append(x[c] * r)
            z[c] = z[c] * r
            inv.append(jnp.where(lane < 8 * (b + tall), z[c], 0.0))
        after = b + tall + ahead
        if after < n:
            w = jnp.concatenate([z[c] for c in own], axis=0)
            h = w.astype(bf16).astype(f32)
            m = (w - h).astype(bf16).astype(f32)
            l = w - h - m
            lhs = jnp.concatenate([h, h, m, m, h, l], axis=0).astype(bf16)
            rhs = jnp.concatenate([h, m, h, m, l, h], axis=0).astype(bf16)
            upd = dot(lhs, rhs, 0, 0)
            for c in range(after, n):
                left[c] = jnp.where(done, 0.0, left[c]) - upd[8 * c:8 * c + 8, :]
    return up, inv

def strips(lo, hi):
    spans = []
    while lo < hi:
        end = min(lo + 2 * NB - lo % (2 * NB), hi)
        spans.append((lo, end))
        lo = end
    return spans


def later_work(a_ref, out_ref, t, p, r0, n, width):
    top = r0 + NB
    turned = [left_stack(p.T, 1)]
    flat = right_stack(p, 0)
    pieces = []
    for lo, hi in strips(top + NB, width):
        q = dot(t, right_stack(a_ref[r0:top, lo:hi], 0), 1, 0)
        out_ref[r0:top, lo:hi] = q
        pieces.append((lo, hi, right_stack(q, 0)))
        if lo < n:
            turned.append(left_stack(q.T, 1))
        yield
    full = jnp.concatenate(turned, axis=0)
    for lo, hi, q in pieces:
        end = min(hi, n)
        a_ref[top:end, lo:hi] = a_ref[top:end, lo:hi] - dot(full[:end - top], q, 1, 0)
        yield


def chol_body(a_ref, out_ref, nblk, width):
    n = nblk * NB
    li = lax.broadcasted_iota(jnp.int32, (NB, NB), 1)
    si = lax.broadcasted_iota(jnp.int32, (NB, NB), 0)
    side = None
    for k in range(nblk):
        r0 = k * NB
        rows = [a_ref[r0 + 8 * b:r0 + 8 * b + 8, r0:r0 + NB] for b in range(16)]
        up, inv = factor_block(rows, side)
        if side is not None:
            for _ in side:
                pass
        out_ref[r0:r0 + NB, r0:r0 + NB] = jnp.where(li >= si, jnp.concatenate(up, axis=0), 0.0)
        if r0 > 0:
            out_ref[r0:r0 + NB, 0:r0] = jnp.zeros((NB, r0), f32)
        t = left_stack(jnp.concatenate(inv, axis=0), 1)
        top = r0 + NB
        p = dot(t, right_stack(a_ref[r0:top, top:top + NB], 0), 1, 0)
        out_ref[r0:top, top:top + NB] = p
        if k + 1 < nblk:
            a_ref[top:top + NB, top:top + NB] = a_ref[top:top + NB, top:top + NB] - dot(
                left_stack(p.T, 1), right_stack(p, 0), 1, 0
            )
            side = later_work(a_ref, out_ref, t, p, r0, n, width)


def exact(a, b):
    return lax.dot_general(
        a, b, (((1,), (0,)), ((), ())), precision=lax.Precision.HIGHEST, preferred_element_type=f32
    )


def blocks_of(nblk):
    return [(i, j) for i in range(nblk) for j in range(i, nblk)]


def fetch(pairs, sem):
    copies = [pltpu.make_async_copy(src, dst, sem.at[i]) for i, (src, dst) in enumerate(pairs)]
    for copy in copies:
        copy.start()
    return copies


def row_parts(rows):
    return [pl.ds(r, NB) for r in range(0, rows, NB)]


def arcs_kernel(design_hbm, weight_hbm, obs_hbm, arc_hbm, out_ref, p_ref, design_ref, weight_ref, obs_ref, arc_ref, sem):
    rows, width = design_ref.shape
    pieces, each = out_ref.shape[:2]
    arcs = pieces * each // 2
    parts = row_parts(rows)
    copies = fetch(
        [(weight_hbm, weight_ref), (arc_hbm, arc_ref), (obs_hbm, obs_ref)]
        + [(design_hbm.at[p], design_ref.at[p]) for p in parts],
        sem,
    )
    for copy in copies[:3]:
        copy.wait()
    w = weight_ref[...]
    number = lax.broadcasted_iota(jnp.int32, (arcs, rows), 0)
    member = jnp.where(number == arc_ref[...], w * w, 0.0)
    total = jnp.sum(member, axis=1, keepdims=True)
    obs = jnp.sum(member * obs_ref[...], axis=1, keepdims=True)
    lane = lax.broadcasted_iota(jnp.int32, (arcs, NB), 1)
    tail = jnp.where(lane == 0, obs, jnp.where(lane == 1, total, 0.0))
    ask = jnp.concatenate([member, jnp.broadcast_to(w * w * obs_ref[...], (8, rows))], axis=0)
    sums = None
    for n, p in enumerate(parts):
        copies[3 + n].wait()
        more = exact(ask[:, n * NB:(n + 1) * NB], design_ref[p, :])
        sums = more if sums is None else sums + more
    p_ref[...] = sums[arcs:]
    sums = jnp.concatenate([sums[:arcs], tail], axis=1)
    for n in range(pieces):
        at = n // 2 * each
        out_ref[n] = sums[at:at + each]


def half_kernel(mine, where_ref, tall_ref, flat_ref, p_ref, out_ref):
    width = flat_ref.shape[1]
    deep = flat_ref.shape[0] // 2
    nblk = width // NB
    order = blocks_of(nblk)
    half = len(order) // 2
    core = where_ref[0]

    def one(side):
        wanted = order[side * half:(side + 1) * half]
        for lo in range(0, nblk, 2):
            tops = sorted({i for i, j in wanted if j in (lo, lo + 1)})
            if not tops:
                continue
            cols = sorted({j for i, j in wanted if j in (lo, lo + 1)})
            c0, c1 = cols[0] * NB, cols[-1] * NB + NB
            r0, r1 = tops[0] * NB, tops[-1] * NB + NB
            g = dot(tall_ref[r0:r1, :], flat_ref[:, c0:c1], 1, 0)
            g = g + dot(tall_ref[r0:r1, :deep], flat_ref[deep:, c0:c1], 1, 0)
            for j in cols:
                for i in tops:
                    if (i, j) in wanted:
                        block = g[i * NB - r0:i * NB - r0 + NB, j * NB - c0:j * NB - c0 + NB]
                        at = wanted.index((i, j)) * NB
                        if i == j and i < 2:
                            corner = [p_ref[0:1, r * 64:(r + 1) * 64] for r in range(i * nblk, (i + 1) * nblk)]
                            corner = jnp.concatenate(corner, axis=0)
                            last = jnp.concatenate([corner, block[NB - 8:, 64:]], axis=1)
                            block = jnp.concatenate([block[:NB - 8], last], axis=0)
                        out_ref[at:at + NB, :] = block

    pl.when(core == (0 if mine else 1))(functools.partial(one, 0))
    pl.when(core == (1 if mine else 0))(functools.partial(one, 1))


def first_kernel(
    where_ref, design_ref, weight_ref, prior_ref, prhs_ref, data_ref, out_ref, tall_ref, flat_ref, p_ref
):
    rows, width = design_ref.shape
    prows = prior_ref.shape[0]
    deep = tall_ref.shape[1] // 2
    include = where_ref[1].astype(f32)
    w = weight_ref[...]

    def place(r, z):
        for c in range(0, width, NB):
            h = z[:, c:c + NB].astype(bf16)
            m = (z[:, c:c + NB] - h.astype(f32)).astype(bf16)
            flat_ref[r:r + NB, c:c + NB] = m
            flat_ref[deep + r:deep + r + NB, c:c + NB] = h
            turned = z[:, c:c + NB].T
            h = turned.astype(bf16)
            tall_ref[c:c + NB, r:r + NB] = h
            tall_ref[c:c + NB, deep + r:deep + r + NB] = (turned - h.astype(f32)).astype(bf16)

    for r in range(0, rows, NB):
        column = jnp.broadcast_to(w[:, r:r + NB], (NB, NB)).T
        place(r, design_ref[r:r + NB, :] * jnp.concatenate([column] * (width // NB), axis=1))
    prior = prior_ref[...] * include
    place(rows, jnp.concatenate([prior, jnp.zeros((NB - prows, width), f32)], axis=0))
    p_ref[...] = data_ref[...] + exact(jnp.broadcast_to(prhs_ref[...], (8, prows)), prior)
    half_kernel(False, where_ref, tall_ref, flat_ref, p_ref, out_ref)


def pair_kernel(where_ref, mine_ref, got_ref, arcs_ref, out_ref):
    width = arcs_ref.shape[2] - NB
    nblk = width // NB
    order = blocks_of(nblk)
    half = len(order) // 2
    core = where_ref[0]
    s = arcs_ref[0]
    for r in range(1, arcs_ref.shape[0]):
        s = s + arcs_ref[r]
    s = jnp.concatenate([s, jnp.zeros((8 - s.shape[0], s.shape[1]), f32)], axis=0)
    total = s[:, width + 1:width + 2] + bias_prior
    b = s * lax.rsqrt(jnp.broadcast_to(total, s.shape))
    obs = b[:, width:width + 1]
    p = jnp.sum(b[:, :width] * obs, axis=0, keepdims=True)
    h = b.astype(bf16).astype(f32)
    m = (b - h).astype(bf16).astype(f32)
    l = b - h - m
    lhs = jnp.concatenate([h, h, m, m, h, l], axis=0).astype(bf16)
    rhs = jnp.concatenate([h, m, h, m, l, h], axis=0).astype(bf16)

    def one(side):
        for t in range(half):
            i, j = order[side * half + t]
            part = dot(lhs[:, i * NB:(i + 1) * NB], rhs[:, j * NB:(j + 1) * NB], 0, 0)
            if i == j and i < 2:
                mine_row = [
                    jnp.concatenate([p[:, r * 64:(r + 1) * 64], part[NB - 8 + r % nblk:NB - 8 + r % nblk + 1, 64:]], axis=1)
                    for r in range(i * nblk, (i + 1) * nblk)
                ]
                part = jnp.concatenate([part[:NB - 8]] + mine_row, axis=0)
            out_ref[t * NB:(t + 1) * NB, :] = mine_ref[t * NB:(t + 1) * NB, :] + got_ref[t * NB:(t + 1) * NB, :] - part

    pl.when(core == 0)(functools.partial(one, 0))
    pl.when(core == 1)(functools.partial(one, 1))


def factor_kernel(where_ref, mine_ref, other_ref, out_ref, rhs_ref, a_ref, u_ref):
    n = u_ref.shape[0]
    nblk = n // NB
    order = blocks_of(nblk)
    half = len(order) // 2
    core = where_ref[0]
    first = core == 0
    for t, (i, j) in enumerate(order):
        rows = pl.ds((t % half) * NB, NB)
        a, b = (mine_ref, other_ref) if t < half else (other_ref, mine_ref)
        a_ref[i * NB:(i + 1) * NB, j * NB:(j + 1) * NB] = jnp.where(first, a[rows, :], b[rows, :])
    lane = lax.broadcasted_iota(jnp.int32, (NB, NB), 1)
    for k in range(nblk):
        d = (2 * k // nblk) * NB
        r = d + NB - 8 + (2 * k) % nblk
        line = jnp.concatenate([a_ref[r:r + 1, d:d + 64], a_ref[r + 1:r + 2, d:d + 64]], axis=1)
        a_ref[k * NB:(k + 1) * NB, n:] = jnp.where(lane == 0, jnp.broadcast_to(line, (NB, NB)).T, 0.0)
    chol_body(a_ref, u_ref, nblk, n + NB)
    share = out_ref.shape[0]
    mine = pl.ds(pl.multiple_of(where_ref[1] * share, share), share)
    out_ref[...] = u_ref[mine, :n]
    rhs_ref[...] = u_ref[mine, n:].T[0:1, :]


def call(kernel, name, where, args, outs, scratch, grant, far=False, cost=None):
    return pl.pallas_call(
        kernel,
        out_shape=outs,
        in_specs=([SMEM] if where is not None else []) + [FAR if far else VMEM] * len(args),
        out_specs=jax.tree.map(lambda _: VMEM, outs),
        scratch_shapes=scratch,
        compiler_params=pltpu.CompilerParams(vmem_limit_bytes=grant * 2**20),
        cost_estimate=cost,
        name=name,
    )(*(() if where is None else (where,)), *args)


def like(*shape):
    return jax.ShapeDtypeStruct(shape, f32)


def on_device(design, observed, row_weight, arc_of_row, prior_factor, prior_rhs):
    rows, width = design.shape
    prows = prior_factor.shape[0]
    nz, nc = lax.axis_size(("zh", "zl")), lax.axis_size("core")
    core, z = lax.axis_index("core"), lax.axis_index(("zh", "zl"))
    arcs = 2 * nz * nc
    nblk = width // NB
    half = len(blocks_of(nblk)) // 2 * NB
    include = (lax.axis_index(("x", "yh", "yl")) == 0).astype(jnp.int32)
    weight = row_weight.reshape(1, rows)
    obs = observed.reshape(1, rows)
    arc = arc_of_row.reshape(1, rows)
    nparts = rows // NB
    deep = rows + NB
    here = jnp.stack([core, include]).astype(jnp.int32)
    partial, p_data = call(
        arcs_kernel,
        "arcs",
        None,
        (design, weight, obs, arc),
        (like(nz * nc, 2 * nc, width + NB), like(8, width)),
        [
            pltpu.VMEM((rows, width), f32),
            pltpu.VMEM((1, rows), f32),
            pltpu.VMEM((1, rows), f32),
            pltpu.VMEM((1, rows), jnp.int32),
            pltpu.SemaphoreType.DMA((3 + nparts,)),
        ],
        56,
        far=True,
    )
    owned = lax.all_to_all(partial, ("zh", "zl", "core"), 0, 0, tiled=True)
    work = pl.CostEstimate(flops=2 * 10**11, bytes_accessed=10**7, transcendentals=0)
    send, tall, flat, p = call(
        first_kernel,
        "first",
        here,
        (design, weight, prior_factor, prior_rhs.reshape(1, prows), p_data),
        (
            pltpu.VMEM((half, NB), f32),
            pltpu.VMEM((width, 2 * deep), bf16),
            pltpu.VMEM((2 * deep, width), bf16),
            pltpu.VMEM((8, width), f32),
        ),
        [],
        14,
        cost=work,
    )
    keep = call(
        functools.partial(half_kernel, True), "keep", here, (tall, flat, p), pltpu.VMEM((half, NB), f32), [], 10, cost=work
    )
    swap = [(i, 1 - i) for i in range(nc)]
    got = lax.ppermute(send, "core", swap)
    where = jnp.stack([core, z * nc + core]).astype(jnp.int32)
    v = call(
        pair_kernel, "pair", where, (keep, got, owned), like(half, NB), [], 10
    )
    block = ("x", "yl", "zl")
    nb, ny, nzh = (lax.axis_size(a) for a in (block, "yh", "zh"))
    v = lax.all_to_all(v.reshape(nb, half // nb, NB), block, 0, 0, tiled=True).sum(0)
    v = lax.all_to_all(v.reshape(ny, 1, v.size // ny), "yh", 0, 0, tiled=True).sum(0)
    v = lax.all_to_all(jnp.broadcast_to(v, (ny * nzh, *v.shape)), ("yh", "zh"), 0, 0, tiled=True)
    v = v.reshape(ny, nzh, 1, v.shape[-1])
    v = functools.reduce(jnp.add, [v[:, n] for n in range(nzh)]).reshape(half // nb, NB)
    v = lax.all_to_all(jnp.broadcast_to(v, (nb, *v.shape)), block, 0, 0, tiled=True)
    v = v.reshape(half, NB)
    other = lax.ppermute(v, "core", swap)
    factor, rhs = call(
        factor_kernel,
        "factor",
        where,
        (v, other),
        (like(prows, width), like(1, prows)),
        [pltpu.VMEM((width, width + NB), f32), pltpu.VMEM((width, width + NB), f32)],
        32,
    )
    return factor, rhs.reshape(prows)


def solution(mesh):
    fine = Mesh(mesh.devices.reshape(4, 4, 2, 4, 2, 2), ("x", "yh", "yl", "zh", "zl", "core"))
    dev = ("zh", "zl", "core")
    every = ("x", "yh", "yl") + dev
    placed = (P(every, None), P(every), P(every), P(every, None), P(dev, None), P(dev))
    return jax.shard_map(
        on_device,
        mesh=fine,
        in_specs=placed,
        out_specs=(P(dev, None), P(dev)),
        check_vma=False,
    )
```

```python
import functools

import jax
import jax.numpy as jnp
from jax import lax
from jax.experimental import pallas as pl
from jax.experimental.pallas import tpu as pltpu
from jax.sharding import Mesh
from jax.sharding import PartitionSpec as P

f32 = jnp.float32
bf16 = jnp.bfloat16
NB = 128
bias_prior = 1.0
VMEM = pl.BlockSpec(memory_space=pltpu.VMEM)
FAR = pl.BlockSpec(memory_space=pltpu.HBM)
SMEM = pl.BlockSpec(memory_space=pltpu.SMEM)


def spread(x, i):
    return jnp.broadcast_to(x[i:i+1, :], (8, x.shape[1]))

def across(x, lane):
    return jnp.broadcast_to(x[:, lane:lane+1], (8, 128))

def split(x):
    hi = x.astype(bf16)
    rest = x - hi.astype(f32)
    mid = rest.astype(bf16)
    return hi, mid, (rest - mid.astype(f32)).astype(bf16)

def left_stack(x, axis):
    h, m, l = split(x)
    return jnp.concatenate([h, h, m, m, h, l], axis=axis)

def right_stack(x, axis):
    h, m, l = split(x)
    return jnp.concatenate([h, m, h, m, l, h], axis=axis)

def dot(a, b, ca, cb):
    return lax.dot_general(a, b, (((ca,), (cb,)), ((), ())), preferred_element_type=f32)

def factor_block(rows, side=None, tall=2, ahead=2):
    sub = lax.broadcasted_iota(jnp.int32, (8, 128), 0)
    lane = lax.broadcasted_iota(jnp.int32, (8, 128), 1)
    n = 16
    left = list(rows)
    up, inv = [], []
    for b in range(0, n, tall):
        own = list(range(b, b + tall))
        near = list(range(b + tall, min(b + tall + ahead, n)))
        steps = 8 * tall
        col = [{c: across(left[c], 8 * b + j) for c in own[j // 8:] + near} for j in range(steps)]
        if side is not None:
            next(side, None)
        x = {c: left[c] for c in own}
        y = {c: jnp.where(lane == sub + 8 * c, 1.0, 0.0) for c in own}
        diag = {c: jnp.ones((8, 128), f32) for c in own}
        mults, heads, qs = [], {}, []
        for j in range(steps):
            home = own[j // 8]
            q = 1.0 / spread(col[j][home], j % 8)
            diag[home] = jnp.where(sub == j % 8, q, diag[home])
            scaled = {c: col[j][c] * q for c in own[j // 8:]}
            qs.append(q)
            for k in range(j + 1, steps):
                kh = own[k // 8]
                head = spread(col[j][kh], k % 8)
                heads[j, k] = head
                for c in own[k // 8:]:
                    if k == j + 1 and c == kh:
                        col[k][c] = col[k][c] - (col[j][c] * head) * q
                    else:
                        col[k][c] = col[k][c] - scaled[c] * head
            sx, sy = spread(x[home], j % 8), spread(y[home], j % 8)
            for c in own[j // 8:]:
                m = jnp.where(sub > j % 8, scaled[c], 0.0) if c == home else scaled[c]
                x[c] = x[c] - m * sx
                y[c] = y[c] - m * sy
        for j in range(steps):
            mults.append({c: col[j][c] * qs[j] for c in near})
            for k in range(j + 1, steps):
                for c in near:
                    col[k][c] = col[k][c] - mults[j][c] * heads[j, k]
        done = (lane >= 8 * b) & (lane < 8 * (b + tall))
        z = {c: jnp.where(done, y[c], x[c]) for c in own}
        if near:
            lines = [spread(z[own[j // 8]], j % 8) for j in range(steps)]
        for c in near:
            dx = [mults[j][c] * lines[j] for j in range(steps)]
            while len(dx) > 1:
                dx = [dx[i] + dx[i + 1] for i in range(0, len(dx), 2)]
            left[c] = jnp.where(done, 0.0, left[c]) - dx[0]
        for c in own:
            r = jnp.sqrt(diag[c])
            up.append(x[c] * r)
            z[c] = z[c] * r
            inv.append(jnp.where(lane < 8 * (b + tall), z[c], 0.0))
        after = b + tall + ahead
        if after < n:
            w = jnp.concatenate([z[c] for c in own], axis=0)
            h = w.astype(bf16).astype(f32)
            m = (w - h).astype(bf16).astype(f32)
            l = w - h - m
            lhs = jnp.concatenate([h, h, m, m, h, l], axis=0).astype(bf16)
            rhs = jnp.concatenate([h, m, h, m, l, h], axis=0).astype(bf16)
            upd = dot(lhs, rhs, 0, 0)
            for c in range(after, n):
                left[c] = jnp.where(done, 0.0, left[c]) - upd[8 * c:8 * c + 8, :]
    return up, inv

def strips(lo, hi):
    spans = []
    while lo < hi:
        end = min(lo + 2 * NB - lo % (2 * NB), hi)
        spans.append((lo, end))
        lo = end
    return spans


def later_work(a_ref, out_ref, t, p, r0, n, width):
    top = r0 + NB
    turned = [left_stack(p.T, 1)]
    flat = right_stack(p, 0)
    pieces = []
    for lo, hi in strips(top + NB, width):
        q = dot(t, right_stack(a_ref[r0:top, lo:hi], 0), 1, 0)
        out_ref[r0:top, lo:hi] = q
        pieces.append((lo, hi, right_stack(q, 0)))
        if lo < n:
            turned.append(left_stack(q.T, 1))
        yield
    full = jnp.concatenate(turned, axis=0)
    for lo, hi, q in pieces:
        end = min(hi, n)
        a_ref[top:end, lo:hi] = a_ref[top:end, lo:hi] - dot(full[:end - top], q, 1, 0)
        yield


def chol_body(a_ref, out_ref, nblk, width):
    n = nblk * NB
    li = lax.broadcasted_iota(jnp.int32, (NB, NB), 1)
    si = lax.broadcasted_iota(jnp.int32, (NB, NB), 0)
    side = None
    for k in range(nblk):
        r0 = k * NB
        rows = [a_ref[r0 + 8 * b:r0 + 8 * b + 8, r0:r0 + NB] for b in range(16)]
        up, inv = factor_block(rows, side)
        if side is not None:
            for _ in side:
                pass
        out_ref[r0:r0 + NB, r0:r0 + NB] = jnp.where(li >= si, jnp.concatenate(up, axis=0), 0.0)
        if r0 > 0:
            out_ref[r0:r0 + NB, 0:r0] = jnp.zeros((NB, r0), f32)
        t = left_stack(jnp.concatenate(inv, axis=0), 1)
        top = r0 + NB
        p = dot(t, right_stack(a_ref[r0:top, top:top + NB], 0), 1, 0)
        out_ref[r0:top, top:top + NB] = p
        if k + 1 < nblk:
            a_ref[top:top + NB, top:top + NB] = a_ref[top:top + NB, top:top + NB] - dot(
                left_stack(p.T, 1), right_stack(p, 0), 1, 0
            )
            side = later_work(a_ref, out_ref, t, p, r0, n, width)


def exact(a, b):
    return lax.dot_general(
        a, b, (((1,), (0,)), ((), ())), precision=lax.Precision.HIGHEST, preferred_element_type=f32
    )


def blocks_of(nblk):
    return [(i, j) for i in range(nblk) for j in range(i, nblk)]


def fetch(pairs, sem):
    copies = [pltpu.make_async_copy(src, dst, sem.at[i]) for i, (src, dst) in enumerate(pairs)]
    for copy in copies:
        copy.start()
    return copies


def row_parts(rows):
    return [pl.ds(r, NB) for r in range(0, rows, NB)]


def arcs_kernel(design_hbm, weight_hbm, obs_hbm, arc_hbm, out_ref, p_ref, design_ref, weight_ref, obs_ref, arc_ref, sem):
    rows, width = design_ref.shape
    pieces, each = out_ref.shape[:2]
    arcs = pieces * each // 2
    parts = row_parts(rows)
    copies = fetch(
        [(weight_hbm, weight_ref), (arc_hbm, arc_ref), (obs_hbm, obs_ref)]
        + [(design_hbm.at[p], design_ref.at[p]) for p in parts],
        sem,
    )
    for copy in copies[:3]:
        copy.wait()
    w = weight_ref[...]
    number = lax.broadcasted_iota(jnp.int32, (arcs, rows), 0)
    member = jnp.where(number == arc_ref[...], w * w, 0.0)
    total = jnp.sum(member, axis=1, keepdims=True)
    obs = jnp.sum(member * obs_ref[...], axis=1, keepdims=True)
    lane = lax.broadcasted_iota(jnp.int32, (arcs, NB), 1)
    tail = jnp.where(lane == 0, obs, jnp.where(lane == 1, total, 0.0))
    ask = jnp.concatenate([member, jnp.broadcast_to(w * w * obs_ref[...], (8, rows))], axis=0)
    sums = None
    for n, p in enumerate(parts):
        copies[3 + n].wait()
        more = exact(ask[:, n * NB:(n + 1) * NB], design_ref[p, :])
        sums = more if sums is None else sums + more
    p_ref[...] = sums[arcs:]
    sums = jnp.concatenate([sums[:arcs], tail], axis=1)
    for n in range(pieces):
        at = n // 2 * each
        out_ref[n] = sums[at:at + each]


def half_kernel(mine, where_ref, tall_ref, flat_ref, p_ref, out_ref):
    width = flat_ref.shape[1]
    deep = flat_ref.shape[0] // 2
    nblk = width // NB
    order = blocks_of(nblk)
    half = len(order) // 2
    core = where_ref[0]

    def one(side):
        wanted = order[side * half:(side + 1) * half]
        for lo in range(0, nblk, 2):
            tops = sorted({i for i, j in wanted if j in (lo, lo + 1)})
            if not tops:
                continue
            cols = sorted({j for i, j in wanted if j in (lo, lo + 1)})
            c0, c1 = cols[0] * NB, cols[-1] * NB + NB
            r0, r1 = tops[0] * NB, tops[-1] * NB + NB
            g = dot(tall_ref[r0:r1, :], flat_ref[:, c0:c1], 1, 0)
            g = g + dot(tall_ref[r0:r1, :deep], flat_ref[deep:, c0:c1], 1, 0)
            for j in cols:
                for i in tops:
                    if (i, j) in wanted:
                        block = g[i * NB - r0:i * NB - r0 + NB, j * NB - c0:j * NB - c0 + NB]
                        at = wanted.index((i, j)) * NB
                        if i == j and i < 2:
                            corner = [p_ref[0:1, r * 64:(r + 1) * 64] for r in range(i * nblk, (i + 1) * nblk)]
                            corner = jnp.concatenate(corner, axis=0)
                            last = jnp.concatenate([corner, block[NB - 8:, 64:]], axis=1)
                            block = jnp.concatenate([block[:NB - 8], last], axis=0)
                        out_ref[at:at + NB, :] = block

    pl.when(core == (0 if mine else 1))(functools.partial(one, 0))
    pl.when(core == (1 if mine else 0))(functools.partial(one, 1))


def first_kernel(
    where_ref, design_ref, weight_ref, prior_ref, prhs_ref, data_ref, out_ref, tall_ref, flat_ref, p_ref
):
    rows, width = design_ref.shape
    prows = prior_ref.shape[0]
    deep = tall_ref.shape[1] // 2
    include = where_ref[1].astype(f32)
    w = weight_ref[...]

    def place(r, z):
        for c in range(0, width, NB):
            h = z[:, c:c + NB].astype(bf16)
            m = (z[:, c:c + NB] - h.astype(f32)).astype(bf16)
            flat_ref[r:r + NB, c:c + NB] = m
            flat_ref[deep + r:deep + r + NB, c:c + NB] = h
            turned = z[:, c:c + NB].T
            h = turned.astype(bf16)
            tall_ref[c:c + NB, r:r + NB] = h
            tall_ref[c:c + NB, deep + r:deep + r + NB] = (turned - h.astype(f32)).astype(bf16)

    for r in range(0, rows, NB):
        column = jnp.broadcast_to(w[:, r:r + NB], (NB, NB)).T
        place(r, design_ref[r:r + NB, :] * jnp.concatenate([column] * (width // NB), axis=1))
    prior = prior_ref[...] * include
    place(rows, jnp.concatenate([prior, jnp.zeros((NB - prows, width), f32)], axis=0))
    p_ref[...] = data_ref[...] + exact(jnp.broadcast_to(prhs_ref[...], (8, prows)), prior)
    half_kernel(False, where_ref, tall_ref, flat_ref, p_ref, out_ref)


def pair_kernel(where_ref, mine_ref, got_ref, arcs_ref, out_ref):
    width = arcs_ref.shape[2] - NB
    nblk = width // NB
    order = blocks_of(nblk)
    half = len(order) // 2
    core = where_ref[0]
    s = arcs_ref[0]
    for r in range(1, arcs_ref.shape[0]):
        s = s + arcs_ref[r]
    s = jnp.concatenate([s, jnp.zeros((8 - s.shape[0], s.shape[1]), f32)], axis=0)
    total = s[:, width + 1:width + 2] + bias_prior
    b = s * lax.rsqrt(jnp.broadcast_to(total, s.shape))
    obs = b[:, width:width + 1]
    p = jnp.sum(b[:, :width] * obs, axis=0, keepdims=True)
    h = b.astype(bf16).astype(f32)
    m = (b - h).astype(bf16).astype(f32)
    l = b - h - m
    lhs = jnp.concatenate([h, h, m, m, h, l], axis=0).astype(bf16)
    rhs = jnp.concatenate([h, m, h, m, l, h], axis=0).astype(bf16)

    def one(side):
        for t in range(half):
            i, j = order[side * half + t]
            part = dot(lhs[:, i * NB:(i + 1) * NB], rhs[:, j * NB:(j + 1) * NB], 0, 0)
            if i == j and i < 2:
                mine_row = [
                    jnp.concatenate([p[:, r * 64:(r + 1) * 64], part[NB - 8 + r % nblk:NB - 8 + r % nblk + 1, 64:]], axis=1)
                    for r in range(i * nblk, (i + 1) * nblk)
                ]
                part = jnp.concatenate([part[:NB - 8]] + mine_row, axis=0)
            out_ref[t * NB:(t + 1) * NB, :] = mine_ref[t * NB:(t + 1) * NB, :] + got_ref[t * NB:(t + 1) * NB, :] - part

    pl.when(core == 0)(functools.partial(one, 0))
    pl.when(core == 1)(functools.partial(one, 1))


def factor_kernel(where_ref, mine_ref, other_ref, out_ref, rhs_ref, a_ref, u_ref):
    n = u_ref.shape[0]
    nblk = n // NB
    order = blocks_of(nblk)
    half = len(order) // 2
    core = where_ref[0]
    first = core == 0
    for t, (i, j) in enumerate(order):
        rows = pl.ds((t % half) * NB, NB)
        a, b = (mine_ref, other_ref) if t < half else (other_ref, mine_ref)
        a_ref[i * NB:(i + 1) * NB, j * NB:(j + 1) * NB] = jnp.where(first, a[rows, :], b[rows, :])
    lane = lax.broadcasted_iota(jnp.int32, (NB, NB), 1)
    for k in range(nblk):
        d = (2 * k // nblk) * NB
        r = d + NB - 8 + (2 * k) % nblk
        line = jnp.concatenate([a_ref[r:r + 1, d:d + 64], a_ref[r + 1:r + 2, d:d + 64]], axis=1)
        a_ref[k * NB:(k + 1) * NB, n:] = jnp.where(lane == 0, jnp.broadcast_to(line, (NB, NB)).T, 0.0)
    chol_body(a_ref, u_ref, nblk, n + NB)
    share = out_ref.shape[0]
    mine = pl.ds(pl.multiple_of(where_ref[1] * share, share), share)
    out_ref[...] = u_ref[mine, :n]
    rhs_ref[...] = u_ref[mine, n:].T[0:1, :]


def call(kernel, name, where, args, outs, scratch, grant, far=False, cost=None):
    return pl.pallas_call(
        kernel,
        out_shape=outs,
        in_specs=([SMEM] if where is not None else []) + [FAR if far else VMEM] * len(args),
        out_specs=jax.tree.map(lambda _: VMEM, outs),
        scratch_shapes=scratch,
        compiler_params=pltpu.CompilerParams(vmem_limit_bytes=grant * 2**20),
        cost_estimate=cost,
        name=name,
    )(*(() if where is None else (where,)), *args)


def like(*shape):
    return jax.ShapeDtypeStruct(shape, f32)


def on_device(design, observed, row_weight, arc_of_row, prior_factor, prior_rhs):
    rows, width = design.shape
    prows = prior_factor.shape[0]
    nz, nc = lax.axis_size(("zh", "zl")), lax.axis_size("core")
    core, z = lax.axis_index("core"), lax.axis_index(("zh", "zl"))
    arcs = 2 * nz * nc
    nblk = width // NB
    half = len(blocks_of(nblk)) // 2 * NB
    include = (lax.axis_index(("x", "yh", "yl")) == 0).astype(jnp.int32)
    weight = row_weight.reshape(1, rows)
    obs = observed.reshape(1, rows)
    arc = arc_of_row.reshape(1, rows)
    nparts = rows // NB
    deep = rows + NB
    here = jnp.stack([core, include]).astype(jnp.int32)
    partial, p_data = call(
        arcs_kernel,
        "arcs",
        None,
        (design, weight, obs, arc),
        (like(nz * nc, 2 * nc, width + NB), like(8, width)),
        [
            pltpu.VMEM((rows, width), f32),
            pltpu.VMEM((1, rows), f32),
            pltpu.VMEM((1, rows), f32),
            pltpu.VMEM((1, rows), jnp.int32),
            pltpu.SemaphoreType.DMA((3 + nparts,)),
        ],
        56,
        far=True,
    )
    owned = lax.all_to_all(partial, ("zh", "zl", "core"), 0, 0, tiled=True)
    work = pl.CostEstimate(flops=2 * 10**11, bytes_accessed=10**7, transcendentals=0)
    send, tall, flat, p = call(
        first_kernel,
        "first",
        here,
        (design, weight, prior_factor, prior_rhs.reshape(1, prows), p_data),
        (
            pltpu.VMEM((half, NB), f32),
            pltpu.VMEM((width, 2 * deep), bf16),
            pltpu.VMEM((2 * deep, width), bf16),
            pltpu.VMEM((8, width), f32),
        ),
        [],
        14,
        cost=work,
    )
    keep = call(
        functools.partial(half_kernel, True), "keep", here, (tall, flat, p), pltpu.VMEM((half, NB), f32), [], 10, cost=work
    )
    swap = [(i, 1 - i) for i in range(nc)]
    got = lax.ppermute(send, "core", swap)
    where = jnp.stack([core, z * nc + core]).astype(jnp.int32)
    v = call(
        pair_kernel, "pair", where, (keep, got, owned), like(half, NB), [], 10
    )
    block = ("x", "yl", "zl")
    nb, ny, nzh = (lax.axis_size(a) for a in (block, "yh", "zh"))
    v = lax.all_to_all(v.reshape(nb, half // nb, NB), block, 0, 0, tiled=True).sum(0)
    v = lax.all_to_all(v.reshape(ny, 1, v.size // ny), "yh", 0, 0, tiled=True).sum(0)
    v = lax.all_to_all(jnp.broadcast_to(v, (ny * nzh, *v.shape)), ("yh", "zh"), 0, 0, tiled=True)
    v = v.reshape(ny, nzh, 1, v.shape[-1])
    v = functools.reduce(jnp.add, [v[:, n] for n in range(nzh)]).reshape(half // nb, NB)
    v = lax.all_to_all(jnp.broadcast_to(v, (nb, *v.shape)), block, 0, 0, tiled=True)
    v = v.reshape(half, NB)
    other = lax.ppermute(v, "core", swap)
    factor, rhs = call(
        factor_kernel,
        "factor",
        where,
        (v, other),
        (like(prows, width), like(1, prows)),
        [pltpu.VMEM((width, width + NB), f32), pltpu.VMEM((width, width + NB), f32)],
        32,
    )
    return factor, rhs.reshape(prows)


def solution(mesh):
    fine = Mesh(mesh.devices.reshape(4, 4, 2, 4, 2, 2), ("x", "yh", "yl", "zh", "zl", "core"))
    dev = ("zh", "zl", "core")
    every = ("x", "yh", "yl") + dev
    placed = (P(every, None), P(every), P(every), P(every, None), P(dev, None), P(dev))
    return jax.shard_map(
        on_device,
        mesh=fine,
        in_specs=placed,
        out_specs=(P(dev, None), P(dev)),
        check_vma=False,
    )
```
